128 devices in a mesh: dp: 16 (over x_hi, y, core), group: 8 (over z, x_lo).
Axes of the slice: x: 4 (x_hi: 2, x_lo: 2; x = x_hi * 2 + x_lo), y: 4, z: 4, core: 2. Of those that a mesh axis runs over, the one named last changes fastest.
Arguments:
- grad_parts: bfloat16 [16, 8, 4194304], P('dp', 'group'), may hold values from -3 to 3
- master_weights: float32 [8, 4194304], P('group', 'dp'), may hold values from -6 to 6
- first_moment: float32 [8, 4194304], P('group', 'dp'), may hold values from -6 to 6
- second_moment: float32 [8, 4194304], P('group', 'dp'), may hold values from 0.25 to 4
- cauchy_points: int32 [10], replicated, may hold values from 1 to 16, as said below
- parity_holder: int32 [16, 8], P('dp'), may hold values from 0 to 7, each once within a row
Outputs:
- new_master: float32 [8, 4194304], P('group', 'dp')
- new_first: float32 [8, 4194304], P('group', 'dp')
- new_second: float32 [8, 4194304], P('group', 'dp')
- parity_shard: float32 [16, 8, 2, 3, 32768], P('dp', 'group')
The draws below stay inside these ranges and needn't reach their ends.
Inputs may be any that keep to these rules, and one draw needn't show every extreme that they name: `cauchy_points`: 10 distinct integers; 1 and 16 are always among them. `parity_holder`: each row is a permutation of 0..7.
All inputs are finite; a program needn't handle non-finite values.
Results may differ from the reference program's by a relative error of at most 0.0003.
Values sent between devices are 32-bit elements; how exact they have to be, the bound alone decides.
No kernel may reach another device: no remote copies, remote signals or barrier semaphores. Data moves between devices by JAX's collectives and lax.ppermute only.
A program may use at most 128 MiB of HBM per device.

```python
import math
import jax
import jax.numpy as jnp
from jax import lax

STEP = 10
G = 8
PARAMS = 4194304
PIECE = 32768
N_DP = 16


def draw_cauchy_points(key, part):
    key = jax.random.fold_in(key, 5)
    inner = jax.random.permutation(key, 14)[:G] + 2
    points = jnp.concatenate([jnp.array([1, 16], jnp.int32), inner.astype(jnp.int32)])
    order_key = jax.random.fold_in(key, 11)
    return jax.random.permutation(order_key, points).astype(jnp.int32)


def draw_grad_parts(key, part):
    key = jax.random.fold_in(key, 7)
    sign_key, size_key, noise_key = jax.random.split(key, 3)
    signs = (2 * jax.random.randint(sign_key, (1, 1, PARAMS), 0, 2) - 1).astype(jnp.float32)
    lowest = 0.05
    highest = 2.5
    noise = 0.25 * jax.random.truncated_normal(noise_key, -4.0, 4.0, (N_DP, G, PARAMS), jnp.float32)
    exponent = jax.random.uniform(size_key, (1, G, PARAMS), jnp.float32, jnp.log(lowest), jnp.log(highest))
    values = signs * jnp.exp(exponent) + noise
    return jnp.clip(values, -3.0, 3.0).astype(jnp.float32).astype(jnp.bfloat16)


def levels(own_key, extent, shards, low, high):
    def one(dim, blocks):
        steps = jax.random.uniform(jax.random.fold_in(jax.random.fold_in(own_key, 6), dim), (blocks,), jnp.float32, low / len(shards), high / len(shards))
        return jnp.repeat(jnp.exp(steps), extent[dim] // blocks).reshape((-1,) + (1,) * (len(extent) - dim - 1))

    gain = one(*shards[0])
    for cut in shards[1:]:
        gain = gain * one(*cut)
    return gain


def normal_values(stream_key, shape, spread, bound, pieces=(), held_as=jnp.bfloat16):
    entries = spread * jax.random.normal(stream_key, shape, jnp.float32)
    if pieces:
        entries = entries * levels(stream_key, shape, pieces, -0.22, 0.18)
    return jnp.clip(entries, -bound, bound).astype(held_as)


def setup_inputs(seed: int = 0) -> dict:
    keys = jax.random.split(jax.random.key(seed), 7)
    grad_parts = draw_grad_parts(jax.random.fold_in(keys[6], 71), 0)
    master_weights = normal_values(keys[1], (G, PARAMS), 1.0, 6.0, ((0, 8), (1, 16)), jnp.float32)
    first_moment = normal_values(keys[2], (G, PARAMS), 2.0, 6.0, ((0, 8), (1, 16)), jnp.float32)
    second_moment = jnp.clip(jnp.exp(math.log(4.0) - 2.7725887 * jax.random.uniform(keys[3], (G, PARAMS), jnp.float32) ** levels(keys[3], (G, PARAMS), ((0, 8), (1, 16)), -0.2, 0.2)), 0.25, 4.0)
    cauchy_points = draw_cauchy_points(jax.random.fold_in(keys[6], 71), 0)
    parity_holder = jax.vmap(lambda own: jax.random.permutation(own, G))(jax.random.split(keys[5], N_DP)).reshape((N_DP, G)).astype(jnp.int32)
    return dict(grad_parts=grad_parts, master_weights=master_weights, first_moment=first_moment, second_moment=second_moment, cauchy_points=cauchy_points, parity_holder=parity_holder)


def reference(grad_parts, master_weights, first_moment, second_moment, cauchy_points, parity_holder):

    def add_part(index, total):
        return total + grad_parts[index].astype(jnp.float32)
    grad = lax.fori_loop(0, N_DP, add_part, jnp.zeros((G, PARAMS), jnp.float32))
    new_first = 0.9 * first_moment + 0.1 * grad
    new_second = 0.95 * second_moment + 0.05 * grad * grad
    first_hat = new_first / (1.0 - 0.9 ** STEP)
    second_hat = new_second / (1.0 - 0.95 ** STEP)
    new_master = master_weights - 0.01 * (first_hat / (jnp.sqrt(second_hat) + 1e-08) + 0.1 * master_weights)
    points = cauchy_points.astype(jnp.float32)
    coeff = 1.0 / (points[:2][:, None] + points[2:][None, :])
    states = jnp.stack([new_master, new_first, new_second], axis=1)
    states = states.reshape(G, 3, N_DP, G, PIECE)
    parity = jnp.einsum('kg,gsdjq->dksjq', coeff, states, precision=lax.Precision.HIGHEST)
    onehot = (parity_holder[:, :, None] == jnp.arange(G, dtype=jnp.int32)[None, None, :]).astype(jnp.int32)
    inverse = lax.optimization_barrier(jnp.sum(onehot * jnp.arange(G, dtype=jnp.int32)[None, :, None], axis=1)).astype(jnp.int32)

    def place(block, order):
        return jnp.take(block, order, axis=2)
    placed = jax.vmap(place)(parity, inverse)
    return (new_master, new_first, new_second, jnp.transpose(placed, (0, 3, 1, 2, 4)))
```

```python
import functools

import jax
import jax.numpy as jnp
from jax import lax
from jax.experimental import pallas as pl
from jax.experimental.pallas import tpu as pltpu
from jax.sharding import PartitionSpec as P

STEP = 10
X, Y, C = 2, 4, 2
G = 8
ROWS = 256
LANES = 128
SHARD = G * ROWS * LANES
CHUNKS = ((0, 64, False), (64, 64, False), (128, 64, False), (192, 64, True))
VMEM = 16 * 2**20


def dp_index(x, y, c):
    return (x * Y + y) * C + c


def dp_perm(move):
    return [
        (dp_index(x, y, c), dp_index(*move(x, y, c)))
        for x in range(X)
        for y in range(Y)
        for c in range(C)
    ]


CORE_SWAP = dp_perm(lambda x, y, c: (x, y, 1 - c))
X_SWAP = dp_perm(lambda x, y, c: (1 - x, y, c))
Y_RING = dp_perm(lambda x, y, c: (x, (y + (1 if c == 0 else -1)) % Y, c))


def params():
    return pltpu.CompilerParams(vmem_limit_bytes=VMEM)


def grad_specs(rows, chunk):
    return [
        pl.BlockSpec(
            (1, 1, rows * LANES),
            lambda i, t, j=j: (0, 0, (t[i] * G + j) * (ROWS // rows) + chunk),
        )
        for j in range(G)
    ]


def widen_kernel(rows, t, *refs):
    out = refs[-1]
    for j in range(G):
        out[0, j] = refs[j][0].astype(jnp.float32).reshape(rows, LANES)


def widen(grad, table, start, rows):
    return pl.pallas_call(
        functools.partial(widen_kernel, rows),
        grid_spec=pltpu.PrefetchScalarGridSpec(
            num_scalar_prefetch=1,
            grid=(X * Y,),
            in_specs=grad_specs(rows, start // rows),
            out_specs=pl.BlockSpec((1, G, rows, LANES), lambda i, t: (i, 0, 0, 0)),
        ),
        out_shape=jax.ShapeDtypeStruct((X * Y, G, rows, LANES), jnp.float32),
        compiler_params=params(),
    )(table, *[grad] * G)


def add_kernel(rows, each, t, *refs):
    got = refs[G]
    outs = refs[G + 1 :]
    step = pl.program_id(0)
    for n, out in enumerate(outs):

        @pl.when(step // each == n)
        def _():
            for j in range(G):
                out[0, j] = refs[j][0].astype(jnp.float32).reshape(rows, LANES) + got[0, j]


def add_core(grad, got, table, start, rows, parts):
    each = X * Y // parts
    return pl.pallas_call(
        functools.partial(add_kernel, rows, each),
        grid_spec=pltpu.PrefetchScalarGridSpec(
            num_scalar_prefetch=1,
            grid=(X * Y,),
            in_specs=grad_specs(rows, start // rows)
            + [pl.BlockSpec((1, G, rows, LANES), lambda i, t: (i, 0, 0, 0))],
            out_specs=[
                pl.BlockSpec(
                    (1, G, rows, LANES),
                    lambda i, t, n=n: (jnp.clip(i - n * each, 0, each - 1), 0, 0, 0),
                )
                for n in range(parts)
            ],
        ),
        out_shape=[jax.ShapeDtypeStruct((each, G, rows, LANES), jnp.float32)] * parts,
        compiler_params=params(),
    )(table, *[grad] * G, got)


def adam_kernel(terms, holder, *refs):
    parts, rest = refs[:terms], refs[terms:]
    master, first, second = rest[:3]
    new_master, new_first, new_second, ordered = rest[-4:]
    for j in range(G):
        grad = parts[0][0, j]
        for part in parts[1:]:
            grad = grad + part[0, j]
        old = master[j]
        m = 0.9 * first[j] + 0.1 * grad
        v = 0.95 * second[j] + 0.05 * grad * grad
        first_hat = m / (1.0 - 0.9**STEP)
        second_hat = v / (1.0 - 0.95**STEP)
        w = old - 0.01 * (first_hat / (jnp.sqrt(second_hat) + 1e-08) + 0.1 * old)
        new_master[j] = w
        new_first[j] = m
        new_second[j] = v
        to = holder[j]
        ordered[to, 0] = w
        ordered[to, 1] = m
        ordered[to, 2] = v


def adam(parts, state, done, holder, start, rows):
    chunk = start // rows
    block = pl.BlockSpec((G, rows, LANES), lambda i, h: (0, chunk, 0))
    term = pl.BlockSpec((1, G, rows, LANES), lambda i, h: (0, 0, 0, 0))
    whole = jax.ShapeDtypeStruct((G, ROWS, LANES), jnp.float32)
    held = list(done or ())
    first_alias = 1 + len(parts) + 3
    return pl.pallas_call(
        functools.partial(adam_kernel, len(parts)),
        grid_spec=pltpu.PrefetchScalarGridSpec(
            num_scalar_prefetch=1,
            grid=(1,),
            in_specs=[term] * len(parts) + [block] * 3 + [pl.BlockSpec(memory_space=pl.ANY)] * len(held),
            out_specs=[block] * 3 + [pl.BlockSpec((G, 3, rows, LANES), lambda i, h: (0, 0, 0, 0))],
        ),
        out_shape=[whole] * 3 + [jax.ShapeDtypeStruct((G, 3, rows, LANES), jnp.float32)],
        input_output_aliases={first_alias + n: n for n in range(len(held))},
        compiler_params=params(),
    )(holder, *parts, *state, *held)


def parity_kernel(coeff, got, *refs):
    out = refs[-1]
    for s in range(3):
        terms = [got[g, s] for g in range(G)]
        for k in range(2):
            total = coeff[k, 0] * terms[0]
            for g in range(1, G):
                total = total + coeff[k, g] * terms[g]
            out[k, s] = total


def parity(got, coeff, done, start, rows):
    chunk = start // rows
    held = [] if done is None else [done]
    return pl.pallas_call(
        parity_kernel,
        grid_spec=pltpu.PrefetchScalarGridSpec(
            num_scalar_prefetch=1,
            grid=(1,),
            in_specs=[pl.BlockSpec((G, 3, rows, LANES), lambda i, c: (0, 0, 0, 0))]
            + [pl.BlockSpec(memory_space=pl.ANY)] * len(held),
            out_specs=pl.BlockSpec((2, 3, rows, LANES), lambda i, c: (0, 0, chunk, 0)),
        ),
        out_shape=jax.ShapeDtypeStruct((2, 3, ROWS, LANES), jnp.float32),
        input_output_aliases={2: 0} if held else {},
        compiler_params=params(),
    )(coeff, got, *held)


def per_device(
    grad_parts, master_weights, first_moment, second_moment, cauchy_points, parity_holder
):
    index = lax.axis_index("dp")
    core, y, x = index % C, (index // C) % Y, index // (C * Y)
    holder = parity_holder.reshape(G)
    state = [a.reshape(G, ROWS, LANES) for a in (master_weights, first_moment, second_moment)]
    points = cauchy_points.astype(jnp.float32)
    coeff = 1.0 / (points[:2][:, None] + points[2:][None, :])

    def table(of_core, x_first):
        way = 1 - 2 * of_core
        steps = jnp.arange(1, Y + 1, dtype=jnp.int32)
        ys = (y - steps * way) % Y
        if x_first:
            xs = jnp.stack([1 - x, x])
            return (((xs[:, None] * Y + ys[None, :]) * C) + of_core).reshape(X * Y)
        xs = jnp.stack([x, 1 - x])
        return (((xs[None, :] * Y + ys[:, None]) * C) + of_core).reshape(X * Y)

    sends = {f: table(1 - core, f).astype(jnp.int32) for f in (False, True)}
    keeps = {f: table(core, f).astype(jnp.int32) for f in (False, True)}

    wide = [widen(grad_parts, sends[f], s, r) for s, r, f in CHUNKS]
    got = [lax.ppermute(w, "dp", CORE_SWAP) for w in wide]
    done, shards = None, None
    for (start, rows, x_first), theirs in zip(CHUNKS, got):
        sums = add_core(grad_parts, theirs, keeps[x_first], start, rows, 2 if x_first else Y)
        if x_first:
            across = lax.ppermute(sums[0], "dp", X_SWAP)
            sums = [sums[1][i : i + 1] + across[i : i + 1] for i in range(Y)]
        running = sums[0]
        for i in range(1, Y):
            running = lax.ppermute(running, "dp", Y_RING)
            if i < Y - 1:
                running = running + sums[i]
        parts = [running, sums[Y - 1]]
        if not x_first:
            parts.append(lax.ppermute(running[1:] + sums[Y - 1][1:], "dp", X_SWAP))
        *done, ordered = adam(parts, state, done, holder, start, rows)
        members = lax.all_to_all(ordered, "group", 0, 0)
        shards = parity(members, coeff, shards, start, rows)
    outs = [a.reshape(1, SHARD) for a in done]
    return (*outs, shards.reshape(1, 1, 2, 3, ROWS * LANES))


def solution(mesh):
    in_specs = (
        P("dp", "group", None),
        P("group", "dp"),
        P("group", "dp"),
        P("group", "dp"),
        P(),
        P("dp", None),
    )
    out_specs = (
        P("group", "dp"),
        P("group", "dp"),
        P("group", "dp"),
        P("dp", "group", None, None, None),
    )
    return jax.shard_map(
        per_device, mesh=mesh, in_specs=in_specs, out_specs=out_specs, check_vma=False
    )
```

```python
import functools

import jax
import jax.numpy as jnp
from jax import lax
from jax.experimental import pallas as pl
from jax.experimental.pallas import tpu as pltpu
from jax.sharding import PartitionSpec as P

STEP = 10
X, Y, C = 2, 4, 2
G = 8
ROWS = 256
LANES = 128
SHARD = G * ROWS * LANES
CHUNKS = ((0, 96, False), (96, 96, False), (192, 64, True))
VMEM = 16 * 2**20


def dp_index(x, y, c):
    return (x * Y + y) * C + c


def dp_perm(move):
    return [
        (dp_index(x, y, c), dp_index(*move(x, y, c)))
        for x in range(X)
        for y in range(Y)
        for c in range(C)
    ]


CORE_SWAP = dp_perm(lambda x, y, c: (x, y, 1 - c))
X_SWAP = dp_perm(lambda x, y, c: (1 - x, y, c))
Y_RING = dp_perm(lambda x, y, c: (x, (y + (1 if c == 0 else -1)) % Y, c))


def params():
    return pltpu.CompilerParams(vmem_limit_bytes=VMEM)


def cost(size):
    return pl.CostEstimate(flops=0, transcendentals=0, bytes_accessed=size // 4096)


def in_hbm(value):
    return pltpu.with_memory_space_constraint(value, pltpu.HBM)


def in_vmem(value):
    return pltpu.with_memory_space_constraint(value, pltpu.VMEM)


def after(value, *others):
    return lax.optimization_barrier((value, *others))[0]


def combine_kernel(rows, start, first, count, offsets, splits, table, grad, *refs):
    terms, refs = refs[: len(offsets)], refs[len(offsets) :]
    outs, (held, sems) = refs[: len(splits)], refs[len(splits) :]
    size = rows * LANES
    copies = [
        pltpu.make_async_copy(
            grad.at[pl.ds(pl.multiple_of(table[first + i] * G, G), G), :, pl.ds(start * LANES, size)],
            held.at[pl.ds(i * G, G)],
            sems.at[i],
        )
        for i in range(count)
    ]
    for copy in copies:
        copy.start()
    places = [(out, i) for out, n in zip(outs, splits) for i in range(n)]
    for i, (copy, (out, at)) in enumerate(zip(copies, places)):
        copy.wait()
        for j in range(G):
            total = held[i * G + j].astype(jnp.float32).reshape(rows, LANES)
            for term, offset in zip(terms, offsets):
                total = total + term[offset + i, j]
            out[at, j] = total


def combine(grad, table, first, splits, terms, start, rows):
    count = sum(splits)
    arrays, offsets = [a for a, _ in terms], tuple(o for _, o in terms)
    return pl.pallas_call(
        functools.partial(combine_kernel, rows, start, first, count, offsets, splits),
        grid_spec=pltpu.PrefetchScalarGridSpec(
            num_scalar_prefetch=1,
            grid=(),
            in_specs=[pl.BlockSpec(memory_space=pl.ANY)]
            + [pl.BlockSpec(memory_space=pltpu.VMEM)] * len(arrays),
            out_specs=[pl.BlockSpec(memory_space=pltpu.VMEM)] * len(splits),
            scratch_shapes=[
                pltpu.VMEM((count * G, 1, rows * LANES), jnp.bfloat16),
                pltpu.SemaphoreType.DMA((count,)),
            ],
        ),
        out_shape=[pltpu.VMEM((n, G, rows, LANES), jnp.float32) for n in splits],
        compiler_params=params(),
        cost_estimate=cost(count * G * rows * LANES * (8 + 4 * len(arrays))),
    )(table, in_hbm(grad), *[in_vmem(a) for a in arrays])


def adam_kernel(terms, rows, start, holder, *refs):
    parts, (master, first, second) = refs[:terms], refs[terms : terms + 3]
    *outs, ordered, fresh, sems = refs[-6:]
    copies = []
    for j in range(G):
        grad = parts[0][0, j]
        for part in parts[1:]:
            grad = grad + part[0, j]
        here = pl.ds(start, rows)
        old = master[j, here]
        m = 0.9 * first[j, here] + 0.1 * grad
        v = 0.95 * second[j, here] + 0.05 * grad * grad
        first_hat = m / (1.0 - 0.9**STEP)
        second_hat = v / (1.0 - 0.95**STEP)
        fresh[j, 0] = old - 0.01 * (first_hat / (jnp.sqrt(second_hat) + 1e-08) + 0.1 * old)
        fresh[j, 1] = m
        fresh[j, 2] = v
        copies.append(pltpu.make_async_copy(fresh.at[j], ordered.at[holder[j]], sems.at[j, 3]))
        for s in range(3):
            copies.append(pltpu.make_async_copy(fresh.at[j, s], outs[s].at[j, here], sems.at[j, s]))
        for copy in copies[-4:]:
            copy.start()
    for copy in copies:
        copy.wait()


def adam(parts, state, done, holder, start, rows):
    whole = jax.ShapeDtypeStruct((G, ROWS, LANES), jnp.float32)
    held = list(done or ())
    first_alias = 1 + len(parts) + 3
    return pl.pallas_call(
        functools.partial(adam_kernel, len(parts), rows, start),
        grid_spec=pltpu.PrefetchScalarGridSpec(
            num_scalar_prefetch=1,
            grid=(),
            in_specs=[pl.BlockSpec(memory_space=pltpu.VMEM)] * (len(parts) + 3)
            + [pl.BlockSpec(memory_space=pl.ANY)] * len(held),
            out_specs=[pl.BlockSpec(memory_space=pl.ANY)] * 4,
            scratch_shapes=[
                pltpu.VMEM((G, 3, rows, LANES), jnp.float32),
                pltpu.SemaphoreType.DMA((G, 4)),
            ],
        ),
        out_shape=[pltpu.HBM(whole.shape, whole.dtype)] * 3
        + [pltpu.HBM((G, 3, rows, LANES), jnp.float32)],
        input_output_aliases={first_alias + n: n for n in range(len(held))},
        compiler_params=params(),
        cost_estimate=cost(G * rows * LANES * 4 * (len(parts) + 9)),
    )(holder, *[in_vmem(a) for a in (*parts, *state)], *[in_hbm(a) for a in held])


def parity_kernel(coeff, got, *refs):
    out = refs[-1]
    for s in range(3):
        terms = [got[g, s] for g in range(G)]
        for k in range(2):
            total = coeff[k, 0] * terms[0]
            for g in range(1, G):
                total = total + coeff[k, g] * terms[g]
            out[s, :, k, :] = total


def parity(got, coeff, done, start, rows):
    chunk = start // rows
    held = [] if done is None else [done]
    return pl.pallas_call(
        parity_kernel,
        grid_spec=pltpu.PrefetchScalarGridSpec(
            num_scalar_prefetch=1,
            grid=(1,),
            in_specs=[pl.BlockSpec((G, 3, rows, LANES), lambda i, c: (0, 0, 0, 0))]
            + [pl.BlockSpec(memory_space=pl.ANY)] * len(held),
            out_specs=pl.BlockSpec((3, rows, 2, LANES), lambda i, c: (0, chunk, 0, 0)),
        ),
        out_shape=jax.ShapeDtypeStruct((3, ROWS, 2, LANES), jnp.float32),
        input_output_aliases={2: 0} if held else {},
        compiler_params=params(),
        cost_estimate=cost(G * 3 * rows * LANES * 6),
    )(coeff, got, *held)


def per_device(
    grad_parts, master_weights, first_moment, second_moment, cauchy_points, parity_holder
):
    index = lax.axis_index("dp")
    core, y, x = index % C, (index // C) % Y, index // (C * Y)
    holder = parity_holder.reshape(G)
    state = [a.reshape(G, ROWS, LANES) for a in (master_weights, first_moment, second_moment)]
    points = cauchy_points.astype(jnp.float32)
    coeff = 1.0 / (points[:2][:, None] + points[2:][None, :])

    def table(of_core, x_first):
        way = 1 - 2 * of_core
        steps = jnp.arange(1, Y + 1, dtype=jnp.int32)
        ys = (y - steps * way) % Y
        if x_first:
            xs = jnp.stack([1 - x, x])
            return (((xs[:, None] * Y + ys[None, :]) * C) + of_core).reshape(X * Y)
        xs = jnp.stack([x, 1 - x])
        return (((xs[None, :] * Y + ys[:, None]) * C) + of_core).reshape(X * Y)

    grad = grad_parts.reshape(X * Y * C * G, 1, ROWS * LANES)
    sends = {f: table(1 - core, f).astype(jnp.int32) for f in (False, True)}
    keeps = {f: table(core, f).astype(jnp.int32) for f in (False, True)}
    got, runs, done, shards = {}, {}, None, None

    def swap_core(n, parts, *earlier):
        start, rows, x_first = CHUNKS[n]
        got.setdefault(n, [])
        first = sum(g.shape[0] for g in got[n])
        wide = combine(grad, after(sends[x_first], *earlier), first, parts, [], start, rows)
        got[n] += [lax.ppermute(w, "dp", CORE_SWAP) for w in wide]
        return wide[-1]

    def ring(n, i, *earlier):
        start, rows, x_first = CHUNKS[n]
        held = after(keeps[x_first], *earlier)
        running = [(runs[n], 0)] if i else []
        if x_first:
            terms = [(got[n][1], i), (across, i), *running]
            (block,) = combine(grad, held, Y + i, (1,), terms, start, rows)
        elif i < Y - 1:
            (block,) = combine(grad, held, X * i, (X,), [(got[n][i], 0), *running], start, rows)
        else:
            own, block = combine(grad, held, X * i, (1, 1), [(got[n][i], 0), *running], start, rows)
            return own, lax.ppermute(block, "dp", X_SWAP)
        if i == Y - 1:
            return [block]
        runs[n] = lax.ppermute(block, "dp", Y_RING)
        return block

    def update(n, parts):
        nonlocal done
        start, rows, _ = CHUNKS[n]
        *done, ordered = adam(parts, state, done, holder, start, rows)
        return lax.all_to_all(ordered, "group", 0, 0)

    def parities(n, members):
        nonlocal shards
        start, rows, _ = CHUNKS[n]
        shards = parity(members, coeff, shards, start, rows)

    w = swap_core(0, (2,))
    w = swap_core(0, (2, 2, 2), w)
    r = ring(0, 0, w)
    w = swap_core(1, (2, 2, 2, 2), r)
    r = ring(1, 0, w)
    r = ring(0, 1, r)
    w = swap_core(2, (4, 4), r)
    r = ring(1, 1, w)
    start, rows, x_first = CHUNKS[2]
    (theirs,) = combine(grad, after(keeps[True], r), 0, (4,), [(got[2][0], 0)], start, rows)
    across = lax.ppermute(theirs, "dp", X_SWAP)
    r = ring(0, 2, theirs)
    r = ring(1, 2, r)
    p0 = ring(0, 3, r)
    r = ring(2, 0, p0[0])
    m0 = update(0, p0)
    r = ring(2, 1, done[0])
    p1 = ring(1, 3, r)
    r = ring(2, 2, p1[0])
    m1 = update(1, p1)
    parities(0, m0)
    p2 = ring(2, 3, shards, done[0])
    m2 = update(2, p2)
    parities(1, m1)
    parities(2, m2)
    outs = [a.reshape(1, SHARD) for a in done]
    return (*outs, shards.transpose(2, 0, 1, 3).reshape(1, 1, 2, 3, ROWS * LANES))


def solution(mesh):
    in_specs = (
        P("dp", "group", None),
        P("group", "dp"),
        P("group", "dp"),
        P("group", "dp"),
        P(),
        P("dp", None),
    )
    out_specs = (
        P("group", "dp"),
        P("group", "dp"),
        P("group", "dp"),
        P("dp", "group", None, None, None),
    )
    return jax.shard_map(
        per_device, mesh=mesh, in_specs=in_specs, out_specs=out_specs, check_vma=False
    )
```

```python
import functools

import jax
import jax.numpy as jnp
from jax import lax
from jax.experimental import pallas as pl
from jax.experimental.pallas import tpu as pltpu
from jax.sharding import PartitionSpec as P

STEP = 10
X, Y, C = 2, 4, 2
G = 8
ROWS = 256
LANES = 128
SHARD = G * ROWS * LANES
CHUNKS = ((0, 96, False), (96, 96, False), (192, 64, True))
GROUPS = ((0,), (1, 2))
TILE = 32
VMEM = 8 * 2**20


def dp_index(x, y, c):
    return (x * Y + y) * C + c


def dp_perm(move):
    return [
        (dp_index(x, y, c), dp_index(*move(x, y, c)))
        for x in range(X)
        for y in range(Y)
        for c in range(C)
    ]


CORE_SWAP = dp_perm(lambda x, y, c: (x, y, 1 - c))
X_SWAP = dp_perm(lambda x, y, c: (1 - x, y, c))
Y_ON = dp_perm(lambda x, y, c: (x, (y + (1 if c == 0 else -1)) % Y, c))
Y_BACK = dp_perm(lambda x, y, c: (x, (y - (1 if c == 0 else -1)) % Y, c))


def params():
    return pltpu.CompilerParams(vmem_limit_bytes=VMEM)


def cost(size):
    return pl.CostEstimate(flops=0, transcendentals=0, bytes_accessed=size // 4096)


def in_hbm(value):
    return pltpu.with_memory_space_constraint(value, pltpu.HBM)


def in_vmem(value):
    return pltpu.with_memory_space_constraint(value, pltpu.VMEM)


def after(value, *others):
    return lax.optimization_barrier((value, *others))[0]


def combine_kernel(tasks, table, grad, *refs):
    arrays = sum(len(task["offsets"]) for task in tasks)
    pieces = sum(len(task["splits"]) for task in tasks)
    terms, outs, scratch = refs[:arrays], refs[arrays : arrays + pieces], refs[arrays + pieces :]
    work = []
    for n, task in enumerate(tasks):
        held, sems = scratch[2 * n : 2 * n + 2]
        size = task["rows"] * LANES
        copies = [
            pltpu.make_async_copy(
                grad.at[
                    pl.ds(pl.multiple_of(table[task["first"] + i] * G, G), G),
                    :,
                    pl.ds(task["start"] * LANES, size),
                ],
                held.at[pl.ds(i * G, G)],
                sems.at[i],
            )
            for i in range(sum(task["splits"]))
        ]
        for copy in copies:
            copy.start()
        work.append((held, copies))
    for task, (held, copies) in zip(tasks, work):
        mine, terms = terms[: len(task["offsets"])], terms[len(task["offsets"]) :]
        places = [(out, i) for out, n in zip(outs, task["splits"]) for i in range(n)]
        outs = outs[len(task["splits"]) :]
        for i, (copy, (out, at)) in enumerate(zip(copies, places)):
            copy.wait()
            for j in range(G):
                total = held[i * G + j].astype(jnp.float32).reshape(task["rows"], LANES)
                for term, offset in zip(mine, task["offsets"]):
                    if 0 <= offset + i < term.shape[0]:
                        total = total + term[offset + i, j]
                out[at, j] = total


def combine(grad, table, tasks):
    arrays = [a for task in tasks for a, _ in task["terms"]]
    shapes = [(n, task["rows"]) for task in tasks for n in task["splits"]]
    static = [
        {**{k: task[k] for k in ("first", "splits", "start", "rows")}, "offsets": [o for _, o in task["terms"]]}
        for task in tasks
    ]
    scratch = []
    for task in tasks:
        count = sum(task["splits"])
        scratch.append(pltpu.VMEM((count * G, 1, task["rows"] * LANES), jnp.bfloat16))
        scratch.append(pltpu.SemaphoreType.DMA((count,)))
    size = sum(n * G * rows * LANES * 8 for n, rows in shapes) + sum(a.size * 4 for a in arrays)
    outs = pl.pallas_call(
        functools.partial(combine_kernel, static),
        grid_spec=pltpu.PrefetchScalarGridSpec(
            num_scalar_prefetch=1,
            grid=(),
            in_specs=[pl.BlockSpec(memory_space=pl.ANY)]
            + [pl.BlockSpec(memory_space=pltpu.VMEM)] * len(arrays),
            out_specs=[pl.BlockSpec(memory_space=pltpu.VMEM)] * len(shapes),
            scratch_shapes=scratch,
        ),
        out_shape=[pltpu.VMEM((n, G, rows, LANES), jnp.float32) for n, rows in shapes],
        compiler_params=params(),
        cost_estimate=cost(size),
    )(table, in_hbm(grad), *[in_vmem(a) for a in arrays])
    results = []
    for task in tasks:
        results.append(outs[: len(task["splits"])])
        outs = outs[len(task["splits"]) :]
    return results


def order_kernel(holder, *refs):
    (*state, ordered), sems = refs[:-1], refs[-1]
    copies = [
        pltpu.make_async_copy(state[s].at[j], ordered.at[holder[j], s], sems.at[j, s])
        for j in range(G)
        for s in range(3)
    ]
    for copy in copies:
        copy.start()
    for copy in copies:
        copy.wait()


def order_state(state, holder):
    return pl.pallas_call(
        order_kernel,
        grid_spec=pltpu.PrefetchScalarGridSpec(
            num_scalar_prefetch=1,
            grid=(),
            in_specs=[pl.BlockSpec(memory_space=pl.ANY)] * 3,
            out_specs=pl.BlockSpec(memory_space=pl.ANY),
            scratch_shapes=[pltpu.SemaphoreType.DMA((G, 3))],
        ),
        out_shape=pltpu.HBM((G, 3, ROWS, LANES), jnp.float32),
        compiler_params=params(),
        cost_estimate=cost(G * 3 * ROWS * LANES * 8),
    )(holder, *[in_hbm(a) for a in state])


def finish_kernel(terms, first, rows, holder, *refs):
    parts = refs[:terms]
    total, ordered, sems = refs[-3:]
    copies = []
    for j in range(G):
        grad = parts[0][0, j]
        for part in parts[1:]:
            grad = grad + part[0, j]
        total[j] = grad
        copy = pltpu.make_async_copy(
            total.at[j], ordered.at[holder[j], pl.ds(first, rows)], sems.at[j]
        )
        copy.start()
        copies.append(copy)
    for copy in copies:
        copy.wait()


def finish(parts, ordered, holder, first, rows, group_rows):
    held = [] if ordered is None else [in_hbm(ordered)]
    return pl.pallas_call(
        functools.partial(finish_kernel, len(parts), first, rows),
        grid_spec=pltpu.PrefetchScalarGridSpec(
            num_scalar_prefetch=1,
            grid=(),
            in_specs=[pl.BlockSpec(memory_space=pltpu.VMEM)] * len(parts)
            + [pl.BlockSpec(memory_space=pl.ANY)] * len(held),
            out_specs=[
                pl.BlockSpec(memory_space=pltpu.VMEM),
                pl.BlockSpec(memory_space=pl.ANY),
            ],
            scratch_shapes=[pltpu.SemaphoreType.DMA((G,))],
        ),
        out_shape=[
            pltpu.VMEM((G, rows, LANES), jnp.float32),
            pltpu.HBM((G, group_rows, LANES), jnp.float32),
        ],
        input_output_aliases={1 + len(parts): 1} if held else {},
        compiler_params=params(),
        cost_estimate=cost(G * rows * LANES * 4 * (len(parts) + 2)),
    )(holder, *[in_vmem(a) for a in parts], *held)


def adam_step(grad, old, first, second):
    m = 0.9 * first + 0.1 * grad
    v = 0.95 * second + 0.05 * grad * grad
    first_hat = m / (1.0 - 0.9**STEP)
    second_hat = v / (1.0 - 0.95**STEP)
    w = old - 0.01 * (first_hat / (jnp.sqrt(second_hat) + 1e-08) + 0.1 * old)
    return w, m, v


def adam_kernel(rows, start, total, *refs):
    state, refs = refs[:3], refs[3:]
    *outs, fresh, sems = refs[-5:]
    here = pl.ds(start, rows)
    copies = []
    for j in range(G):
        for s, value in enumerate(adam_step(total[j], *[a[j, here] for a in state])):
            fresh[s, j] = value
            copy = pltpu.make_async_copy(fresh.at[s, j], outs[s].at[j, here], sems.at[j, s])
            copy.start()
            copies.append(copy)
    for copy in copies:
        copy.wait()


def adam(total, state, done, start, rows):
    held = [in_hbm(a) for a in done or ()]
    return pl.pallas_call(
        functools.partial(adam_kernel, rows, start),
        grid_spec=pltpu.PrefetchScalarGridSpec(
            num_scalar_prefetch=0,
            grid=(),
            in_specs=[pl.BlockSpec(memory_space=pltpu.VMEM)] * 4
            + [pl.BlockSpec(memory_space=pl.ANY)] * len(held),
            out_specs=[pl.BlockSpec(memory_space=pl.ANY)] * 3,
            scratch_shapes=[
                pltpu.VMEM((3, G, rows, LANES), jnp.float32),
                pltpu.SemaphoreType.DMA((G, 3)),
            ],
        ),
        out_shape=[pltpu.HBM((G, ROWS, LANES), jnp.float32)] * 3,
        input_output_aliases={4 + n: n for n in range(len(held))},
        compiler_params=params(),
        cost_estimate=cost(G * rows * LANES * 4 * 7),
    )(in_vmem(total), *[in_vmem(a) for a in state], *held)


def parity_kernel(coeff, sums, old, *refs):
    out = refs[-1]
    totals = [[None] * 2 for _ in range(3)]
    for g in range(G):
        for s, value in enumerate(adam_step(sums[g], *[old[g, s] for s in range(3)])):
            for k in range(2):
                term = coeff[k, g] * value
                totals[s][k] = term if g == 0 else totals[s][k] + term
    for s in range(3):
        for k in range(2):
            out[s, :, k, :] = totals[s][k]


def parity(sums, old, coeff, done, start, rows):
    first = start // TILE
    held = [] if done is None else [in_hbm(done)]
    return pl.pallas_call(
        parity_kernel,
        grid_spec=pltpu.PrefetchScalarGridSpec(
            num_scalar_prefetch=1,
            grid=(rows // TILE,),
            in_specs=[
                pl.BlockSpec((G, TILE, LANES), lambda i, c: (0, i, 0)),
                pl.BlockSpec((G, 3, TILE, LANES), lambda i, c: (0, 0, first + i, 0)),
            ]
            + [pl.BlockSpec(memory_space=pl.ANY)] * len(held),
            out_specs=pl.BlockSpec((3, TILE, 2, LANES), lambda i, c: (0, first + i, 0, 0)),
        ),
        out_shape=pltpu.HBM((3, ROWS, 2, LANES), jnp.float32),
        input_output_aliases={3: 0} if held else {},
        compiler_params=params(),
        cost_estimate=cost(G * 4 * rows * LANES * 4),
    )(coeff, sums, old, *held)


def per_device(
    grad_parts, master_weights, first_moment, second_moment, cauchy_points, parity_holder
):
    index = lax.axis_index("dp")
    core, y, x = index % C, (index // C) % Y, index // (C * Y)
    holder = parity_holder.reshape(G)
    state = [a.reshape(G, ROWS, LANES) for a in (master_weights, first_moment, second_moment)]
    points = cauchy_points.astype(jnp.float32)
    coeff = 1.0 / (points[:2][:, None] + points[2:][None, :])

    def table(of_core, x_first):
        way = 1 - 2 * of_core
        ys = jnp.stack([y + 2, y - way, y + way, y]) % Y
        if x_first:
            xs = jnp.stack([1 - x, x])
            return (((xs[:, None] * Y + ys[None, :]) * C) + of_core).reshape(X * Y)
        xs = jnp.stack([x, 1 - x])
        return (((xs[None, :] * Y + ys[:, None]) * C) + of_core).reshape(X * Y)

    grad = grad_parts.reshape(X * Y * C * G, 1, ROWS * LANES)
    tables = [table(1 - core, False), table(1 - core, True), table(core, False), table(core, True)]
    blocks = jnp.concatenate(tables).astype(jnp.int32)
    half = X * Y // 2
    got = {n: [] for n in range(len(CHUNKS))}
    across = {n: [] for n in range(len(CHUNKS))}
    hop, totals, ordered, olds, done, shards = {}, {}, {}, None, None, None
    token = ()

    def task(n, own, first, splits, terms):
        start, rows, x_first = CHUNKS[n]
        base = X * Y * (2 * own + x_first)
        return dict(first=base + first, start=start, rows=rows, splits=splits, terms=terms)

    def run(*jobs, wait=()):
        nonlocal token
        table = after(blocks, *token, *wait)
        results = combine(grad, table, [job[0] for job in jobs])
        token = (results[0][0],)
        for (_, use), result in zip(jobs, results):
            use(*result)

    def then(*values):
        nonlocal token
        token = values

    def swap_core(n, part, splits=(2, 2)):
        def use(*sent):
            got[n] += [lax.ppermute(a, "dp", CORE_SWAP) for a in sent]

        return task(n, False, half * part, splits, []), use

    def offsets(arrays, first):
        pairs, at = [], 0
        for a in arrays:
            pairs.append((a, first - at))
            at += a.shape[0]
        return pairs

    def of_core(n, first):
        return offsets(got[n], first)

    def of_x(n, first):
        return offsets(across[n], first - half)

    def x_sum(n):
        def use(*sent):
            across[n] += [lax.ppermute(a, "dp", X_SWAP) for a in sent]

        return task(n, True, 0, (2, 2), of_core(n, 0)), use

    def terms_at(n, first, count):
        terms = of_core(n, first) + (of_x(n, first) if CHUNKS[n][2] else [])
        return [(a, o) for a, o in terms if o < a.shape[0] and o + count > 0]

    def step_1(n):
        first, size = (half, 1) if CHUNKS[n][2] else (0, X)

        def use(far, near):
            hop[n, 0] = lax.ppermute(far, "dp", Y_ON)
            hop[n, 1] = lax.ppermute(near, "dp", Y_BACK)

        return task(n, True, first, (size, size), terms_at(n, first, 2 * size)), use

    def step_2(n):
        first, size = (half + 2, 1) if CHUNKS[n][2] else (half, X)

        def use(block):
            hop[n, 2] = lax.ppermute(block, "dp", Y_ON)

        return task(n, True, first, (size,), terms_at(n, first, size) + [(hop[n, 0], 0)]), use

    def step_3(n):
        first, splits = (half + 3, (1,)) if CHUNKS[n][2] else (half + X, (1, 1))

        def use(own, *block):
            totals[n] = [own] + [lax.ppermute(b, "dp", X_SWAP) for b in block]

        terms = terms_at(n, first, len(splits)) + [(hop[n, 2], 0), (hop[n, 1], 0)]
        return task(n, True, first, splits, terms), use

    def give(n):
        (group,) = [g for g in GROUPS if n in g]
        base = min(CHUNKS[m][0] for m in group)
        start, rows, _ = CHUNKS[n]
        totals[n], ordered[group] = finish(
            totals[n],
            ordered.get(group),
            after(holder, *token),
            start - base,
            rows,
            sum(CHUNKS[m][1] for m in group),
        )
        then(totals[n])

    def to_holders(group):
        ordered[group] = lax.all_to_all(ordered[group], "group", 0, 0)

    def update(n):
        nonlocal done
        start, rows, _ = CHUNKS[n]
        done = adam(after(totals[n], *token), state, done, start, rows)
        then(done[0])

    def parities(group):
        nonlocal shards
        start = min(CHUNKS[m][0] for m in group)
        rows = sum(CHUNKS[m][1] for m in group)
        shards = parity(ordered[group], olds, after(coeff, *token), shards, start, rows)
        then(shards)

    run(swap_core(0, 0))
    run(swap_core(2, 0))
    run(step_1(0))
    run(x_sum(2))
    old = order_state(state, after(holder, *token))
    then(old)
    olds = lax.all_to_all(old, "group", 0, 0)
    run(swap_core(0, 1, (1, 1, 1, 1)), swap_core(1, 0))
    run(step_2(0), swap_core(2, 1), wait=(across[2][0],))
    run(step_1(1), swap_core(1, 1), wait=(hop[0, 1],))
    run(step_3(0), wait=(across[2][1],))
    run(step_2(1))
    then(*token, hop[1, 1])
    give(0)
    to_holders((0,))
    run(step_1(2), wait=(olds,))
    run(step_3(1))
    run(step_2(2))
    update(0)
    run(step_3(2))
    give(2)
    give(1)
    to_holders((1, 2))
    parities((0,))
    update(1)
    update(2)
    parities((1, 2))
    outs = [a.reshape(1, SHARD) for a in done]
    return (*outs, shards.transpose(2, 0, 1, 3).reshape(1, 1, 2, 3, ROWS * LANES))


def solution(mesh):
    in_specs = (
        P("dp", "group", None),
        P("group", "dp"),
        P("group", "dp"),
        P("group", "dp"),
        P(),
        P("dp", None),
    )
    out_specs = (
        P("group", "dp"),
        P("group", "dp"),
        P("group", "dp"),
        P("dp", "group", None, None, None),
    )
    return jax.shard_map(
        per_device, mesh=mesh, in_specs=in_specs, out_specs=out_specs, check_vma=False
    )
```

```python
import functools

import jax
import jax.numpy as jnp
import numpy as np
from jax import lax
from jax.experimental import pallas as pl
from jax.experimental.pallas import tpu as pltpu
from jax.sharding import PartitionSpec as P

STEP = 10
X, Y, C = 2, 4, 2
G = 8
ROWS = 256
LANES = 128
SHARD = G * ROWS * LANES
CHUNKS = ((0, 160, False), (160, 96, False))
GROUPS = ((0,), (1,))
TILE = 32
VMEM = 8 * 2**20


def dp_index(x, y, c):
    return (x * Y + y) * C + c


def dp_perm(move):
    return [
        (dp_index(x, y, c), dp_index(*move(x, y, c)))
        for x in range(X)
        for y in range(Y)
        for c in range(C)
    ]


CORE_SWAP = dp_perm(lambda x, y, c: (x, y, 1 - c))
X_SWAP = dp_perm(lambda x, y, c: (1 - x, y, c))
Y_ON = dp_perm(lambda x, y, c: (x, (y + (1 if c == 0 else -1)) % Y, c))
Y_BACK = dp_perm(lambda x, y, c: (x, (y - (1 if c == 0 else -1)) % Y, c))


SHARE = 4096


def params():
    return pltpu.CompilerParams(vmem_limit_bytes=VMEM)


def block_table(x, y, of_core, x_first):
    way = 1 - 2 * of_core
    ys = [(y + step) % Y for step in (2, -way, way, 0)]
    if x_first:
        return [dp_index(at, to, of_core) for at in (1 - x, x) for to in ys]
    return [dp_index(at, to, of_core) for to in ys for at in (x, 1 - x)]


TABLES = np.array(
    [
        sum((block_table(x, y, of, f) for of in (1 - c, c) for f in (False, True)), [])
        for x in range(X)
        for y in range(Y)
        for c in range(C)
    ],
    np.int32,
)


def cost(size):
    return pl.CostEstimate(flops=0, transcendentals=0, bytes_accessed=size // SHARE)


def in_hbm(value):
    return pltpu.with_memory_space_constraint(value, pltpu.HBM)


def in_vmem(value):
    return pltpu.with_memory_space_constraint(value, pltpu.VMEM)


def after(value, *others):
    return lax.optimization_barrier((value, *others))[0]


def combine_kernel(tasks, table, grad, *refs):
    arrays = sum(len(task["offsets"]) for task in tasks)
    pieces = sum(len(task["splits"]) for task in tasks)
    terms, outs, scratch = refs[:arrays], refs[arrays : arrays + pieces], refs[arrays + pieces :]
    work = []
    for n, task in enumerate(tasks):
        held, sems = scratch[2 * n : 2 * n + 2]
        size = task["rows"] * LANES
        copies = [
            pltpu.make_async_copy(
                grad.at[
                    pl.ds(pl.multiple_of(table[task["first"] + i] * G, G), G),
                    :,
                    pl.ds(task["start"] * LANES, size),
                ],
                held.at[pl.ds(i * G, G)],
                sems.at[i],
            )
            for i in range(sum(task["splits"]))
        ]
        for copy in copies:
            copy.start()
        work.append((held, copies))
    for task, (held, copies) in zip(tasks, work):
        mine, terms = terms[: len(task["offsets"])], terms[len(task["offsets"]) :]
        places = [(out, i) for out, n in zip(outs, task["splits"]) for i in range(n)]
        outs = outs[len(task["splits"]) :]
        for i, (copy, (out, at)) in enumerate(zip(copies, places)):
            copy.wait()
            for j in range(G):
                total = held[i * G + j].reshape(task["rows"], LANES).astype(jnp.float32)
                for term, offset in zip(mine, task["offsets"]):
                    if 0 <= offset + i < term.shape[0]:
                        total = total + term[offset + i, j]
                out[at, j] = total


def combine(grad, table, tasks, name):
    arrays = [a for task in tasks for a, _ in task["terms"]]
    shapes = [(n, task["rows"]) for task in tasks for n in task["splits"]]
    static = [
        {**{k: task[k] for k in ("first", "splits", "start", "rows")}, "offsets": [o for _, o in task["terms"]]}
        for task in tasks
    ]
    scratch = []
    for task in tasks:
        count = sum(task["splits"])
        scratch.append(pltpu.VMEM((count * G, 1, task["rows"] * LANES), jnp.bfloat16))
        scratch.append(pltpu.SemaphoreType.DMA((count,)))
    size = sum(n * G * rows * LANES * 8 for n, rows in shapes) + sum(a.size * 4 for a in arrays)
    outs = pl.pallas_call(
        functools.partial(combine_kernel, static),
        grid_spec=pltpu.PrefetchScalarGridSpec(
            num_scalar_prefetch=1,
            grid=(),
            in_specs=[pl.BlockSpec(memory_space=pl.ANY)]
            + [pl.BlockSpec(memory_space=pltpu.VMEM)] * len(arrays),
            out_specs=[pl.BlockSpec(memory_space=pltpu.VMEM)] * len(shapes),
            scratch_shapes=scratch,
        ),
        out_shape=[pltpu.VMEM((n, G, rows, LANES), jnp.float32) for n, rows in shapes],
        name=name,
        compiler_params=params(),
        cost_estimate=cost(size),
    )(table, in_hbm(grad), *[in_vmem(a) for a in arrays])
    results = []
    for task in tasks:
        results.append(outs[: len(task["splits"])])
        outs = outs[len(task["splits"]) :]
    return results


def order_kernel(holder, *refs):
    (*state, ordered), sems = refs[:-1], refs[-1]
    copies = [
        pltpu.make_async_copy(state[s].at[j], ordered.at[holder[j], s], sems.at[j, s])
        for j in range(G)
        for s in range(3)
    ]
    for copy in copies:
        copy.start()
    for copy in copies:
        copy.wait()


def order_state(state, holder):
    return pl.pallas_call(
        order_kernel,
        grid_spec=pltpu.PrefetchScalarGridSpec(
            num_scalar_prefetch=1,
            grid=(),
            in_specs=[pl.BlockSpec(memory_space=pltpu.VMEM)] * 3,
            out_specs=pl.BlockSpec(memory_space=pl.ANY),
            scratch_shapes=[pltpu.SemaphoreType.DMA((G, 3))],
        ),
        out_shape=pltpu.HBM((G, 3, ROWS, LANES), jnp.float32),
        name="order",
        compiler_params=params(),
        cost_estimate=cost(G * 3 * ROWS * LANES * 8),
    )(holder, *[in_vmem(a) for a in state])


def finish_kernel(terms, first, rows, holder, *refs):
    parts = refs[:terms]
    ordered, total, sems = refs[-3:]
    copies = []
    for j in range(G):
        grad = parts[0][0, j]
        for part in parts[1:]:
            grad = grad + part[0, j]
        total[j] = grad
        copy = pltpu.make_async_copy(
            total.at[j], ordered.at[holder[j], pl.ds(first, rows)], sems.at[j]
        )
        copy.start()
        copies.append(copy)
    for copy in copies:
        copy.wait()


def finish(parts, ordered, holder, first, rows, group_rows):
    held = [] if ordered is None else [in_hbm(ordered)]
    return pl.pallas_call(
        functools.partial(finish_kernel, len(parts), first, rows),
        grid_spec=pltpu.PrefetchScalarGridSpec(
            num_scalar_prefetch=1,
            grid=(),
            in_specs=[pl.BlockSpec(memory_space=pltpu.VMEM)] * len(parts)
            + [pl.BlockSpec(memory_space=pl.ANY)] * len(held),
            out_specs=pl.BlockSpec(memory_space=pl.ANY),
            scratch_shapes=[
                pltpu.VMEM((G, rows, LANES), jnp.float32),
                pltpu.SemaphoreType.DMA((G,)),
            ],
        ),
        out_shape=pltpu.HBM((G, group_rows, LANES), jnp.float32),
        name="finish",
        input_output_aliases={1 + len(parts): 0} if held else {},
        compiler_params=params(),
        cost_estimate=cost(G * rows * LANES * 4 * (len(parts) + 2)),
    )(holder, *[in_vmem(a) for a in parts], *held)


def adam_step(grad, old, first, second):
    m = 0.9 * first + 0.1 * grad
    v = 0.95 * second + 0.05 * grad * grad
    first_hat = m / (1.0 - 0.9**STEP)
    second_hat = v / (1.0 - 0.95**STEP)
    w = old - 0.01 * (first_hat / (jnp.sqrt(second_hat) + 1e-08) + 0.1 * old)
    return w, m, v


def adam_kernel(first, rows, start, holder, ordered, *refs):
    state, refs = refs[:3], refs[3:]
    *outs, grads, old, fresh, in_sems, out_sems = refs[-8:]
    here = pl.ds(start, rows)
    loads, stores = [], []
    for j in range(G):
        pairs = [(ordered.at[holder[j], pl.ds(first, rows)], grads.at[j])]
        pairs += [(state[s].at[j, here], old.at[s, j]) for s in range(3)]
        loads.append(
            [pltpu.make_async_copy(*pair, in_sems.at[j, s]) for s, pair in enumerate(pairs)]
        )
        for load in loads[-1]:
            load.start()
    for j in range(G):
        for load in loads[j]:
            load.wait()
        for s, value in enumerate(adam_step(grads[j], *[old[s, j] for s in range(3)])):
            fresh[s, j] = value
            store = pltpu.make_async_copy(fresh.at[s, j], outs[s].at[j, here], out_sems.at[j, s])
            store.start()
            stores.append(store)
    for store in stores:
        store.wait()


def adam(ordered, state, done, holder, first, start, rows):
    held = [in_hbm(a) for a in done or ()]
    return pl.pallas_call(
        functools.partial(adam_kernel, first, rows, start),
        grid_spec=pltpu.PrefetchScalarGridSpec(
            num_scalar_prefetch=1,
            grid=(),
            in_specs=[pl.BlockSpec(memory_space=pl.ANY)] * (4 + len(held)),
            out_specs=[pl.BlockSpec(memory_space=pl.ANY)] * 3,
            scratch_shapes=[
                pltpu.VMEM((G, rows, LANES), jnp.float32),
                pltpu.VMEM((3, G, rows, LANES), jnp.float32),
                pltpu.VMEM((3, G, rows, LANES), jnp.float32),
                pltpu.SemaphoreType.DMA((G, 4)),
                pltpu.SemaphoreType.DMA((G, 3)),
            ],
        ),
        out_shape=[pltpu.HBM((G, ROWS, LANES), jnp.float32)] * 3,
        name="adam",
        input_output_aliases={5 + n: n for n in range(len(held))},
        compiler_params=params(),
        cost_estimate=cost(G * rows * LANES * 4 * 7),
    )(holder, in_hbm(ordered), *[in_hbm(a) for a in state], *held)


def parity_kernel(coeff, sums, old, *refs):
    out = refs[-1]
    totals = [[None] * 2 for _ in range(3)]
    for g in range(G):
        for s, value in enumerate(adam_step(sums[g], *[old[g, s] for s in range(3)])):
            for k in range(2):
                term = coeff[k, g] * value
                totals[s][k] = term if g == 0 else totals[s][k] + term
    for s in range(3):
        for k in range(2):
            out[s, :, k, :] = totals[s][k]


def parity(sums, old, coeff, done, start, rows):
    first = start // TILE
    held = [] if done is None else [in_hbm(done)]
    return pl.pallas_call(
        parity_kernel,
        grid_spec=pltpu.PrefetchScalarGridSpec(
            num_scalar_prefetch=1,
            grid=(rows // TILE,),
            in_specs=[
                pl.BlockSpec((G, TILE, LANES), lambda i, c: (0, i, 0)),
                pl.BlockSpec((G, 3, TILE, LANES), lambda i, c: (0, 0, first + i, 0)),
            ]
            + [pl.BlockSpec(memory_space=pl.ANY)] * len(held),
            out_specs=pl.BlockSpec((3, TILE, 2, LANES), lambda i, c: (0, first + i, 0, 0)),
        ),
        out_shape=pltpu.HBM((3, ROWS, 2, LANES), jnp.float32),
        name="parity",
        input_output_aliases={3: 0} if held else {},
        compiler_params=params(),
        cost_estimate=cost(G * 4 * rows * LANES * 4),
    )(coeff, sums, old, *held)


def per_device(
    grad_parts, master_weights, first_moment, second_moment, cauchy_points, parity_holder
):
    index = lax.axis_index("dp")
    holder = parity_holder.reshape(G)
    state = [a.reshape(G, ROWS, LANES) for a in (master_weights, first_moment, second_moment)]
    points = cauchy_points.astype(jnp.float32)
    coeff = 1.0 / (points[:2][:, None] + points[2:][None, :])

    grad = grad_parts.reshape(X * Y * C * G, 1, ROWS * LANES)
    blocks = lax.dynamic_index_in_dim(jnp.asarray(TABLES), index, keepdims=False)
    half = X * Y // 2
    got = {n: [] for n in range(len(CHUNKS))}
    across = {n: [] for n in range(len(CHUNKS))}
    hop, totals, ordered, sums, olds, done, shards = {}, {}, {}, {}, None, None, None
    token = ()

    def task(n, own, first, splits, terms):
        start, rows, x_first = CHUNKS[n]
        base = X * Y * (2 * own + x_first)
        return dict(first=base + first, start=start, rows=rows, splits=splits, terms=terms)

    def send(value, name, n, pairs):
        with jax.named_scope(f"{name}_{n}"):
            return lax.ppermute(value, "dp", pairs)

    def run(*jobs, wait=()):
        nonlocal token
        table = after(blocks, *token, *wait)
        name = "_".join(f"{job[2]}{job[3]}" for job in jobs)
        results = combine(grad, table, [job[0] for job in jobs], name)
        token = (results[0][0],)
        for (_, use, *_), result in zip(jobs, results):
            use(*result)

    def then(*values):
        nonlocal token
        token = values

    def swap_core(n, first, splits):
        def use(*sent):
            got[n] += [send(a, "core", n, CORE_SWAP) for a in sent]

        return task(n, False, first, splits, []), use, "core", n

    def offsets(arrays, first):
        pairs, at = [], 0
        for a in arrays:
            pairs.append((a, first - at))
            at += a.shape[0]
        return pairs

    def of_core(n, first):
        return offsets(got[n], first)

    def of_x(n, first):
        return offsets(across[n], first - half)

    def x_sum(n):
        def use(*sent):
            across[n] += [send(a, "cross", n, X_SWAP) for a in sent]

        return task(n, True, 0, (2, 2), of_core(n, 0)), use, "cross", n

    def terms_at(n, first, count):
        terms = of_core(n, first) + (of_x(n, first) if CHUNKS[n][2] else [])
        return [(a, o) for a, o in terms if o < a.shape[0] and o + count > 0]

    def far(n):
        first, size = (half, 1) if CHUNKS[n][2] else (0, X)

        def use(block):
            hop[n, 0] = send(block, "far", n, Y_ON)

        return task(n, True, first, (size,), terms_at(n, first, size)), use, "far", n

    def near(n):
        first, size = (half + 1, 1) if CHUNKS[n][2] else (X, X)

        def use(block):
            hop[n, 1] = send(block, "near", n, Y_BACK)

        return task(n, True, first, (size,), terms_at(n, first, size)), use, "near", n

    def ahead(n):
        first, size = (half + 2, 1) if CHUNKS[n][2] else (half, X)

        def use(block):
            hop[n, 2] = send(block, "ahead", n, Y_ON)

        terms = terms_at(n, first, size) + [(hop[n, 0], 0)]
        return task(n, True, first, (size,), terms), use, "ahead", n

    def here(n):
        first, splits = (half + 3, (1,)) if CHUNKS[n][2] else (half + X, (1, 1))

        def use(own, *block):
            totals[n] = [own] + [send(b, "swap", n, X_SWAP) for b in block]

        terms = terms_at(n, first, len(splits)) + [(hop[n, 2], 0), (hop[n, 1], 0)]
        return task(n, True, first, splits, terms), use, "here", n

    def place(n):
        (group,) = [g for g in GROUPS if n in g]
        base = min(CHUNKS[m][0] for m in group)
        return group, CHUNKS[n][0] - base, sum(CHUNKS[m][1] for m in group)

    def give(n):
        group, first, group_rows = place(n)
        rows = CHUNKS[n][1]
        parts, before = totals[n], ordered.get(group)
        ordered[group] = finish(parts, before, after(holder, *token), first, rows, group_rows)
        then(ordered[group])

    def to_holders(group):
        sums[group] = lax.all_to_all(ordered[group], "group", 0, 0)

    def update(n):
        nonlocal done
        group, first, _ = place(n)
        start, rows, _ = CHUNKS[n]
        done = adam(ordered[group], state, done, after(holder, *token), first, start, rows)
        then(done[0])

    def parities(group):
        nonlocal shards
        start = min(CHUNKS[m][0] for m in group)
        rows = sum(CHUNKS[m][1] for m in group)
        shards = parity(sums[group], olds, after(coeff, *token), shards, start, rows)
        then(shards)

    run(swap_core(0, 0, (1, 1)))
    run(swap_core(0, 2, (1, 1)))
    run(far(0))
    old = order_state(state, after(holder, *token))
    then(old)
    olds = lax.all_to_all(old, 'group', 0, 0)
    run(near(0), swap_core(0, 4, (1, 1, 1, 1)))
    run(swap_core(1, 0, (1, 1, 1, 1)), swap_core(1, 4, (1, 1, 1, 1)))
    run(ahead(0))
    run(far(1), wait=(hop[0, 1],))
    run(near(1))
    run(here(0))
    run(ahead(1))
    give(0)
    to_holders((0,))
    run(here(1))
    update(0)
    parities((0,))
    give(1)
    to_holders((1,))
    update(1)
    parities((1,))
    outs = [a.reshape(1, SHARD) for a in done]
    return (*outs, shards.transpose(2, 0, 1, 3).reshape(1, 1, 2, 3, ROWS * LANES))


def solution(mesh):
    in_specs = (
        P("dp", "group", None),
        P("group", "dp"),
        P("group", "dp"),
        P("group", "dp"),
        P(),
        P("dp", None),
    )
    out_specs = (
        P("group", "dp"),
        P("group", "dp"),
        P("group", "dp"),
        P("dp", "group", None, None, None),
    )
    return jax.shard_map(
        per_device, mesh=mesh, in_specs=in_specs, out_specs=out_specs, check_vma=False
    )
```

```python
import functools

import jax
import jax.numpy as jnp
import numpy as np
from jax import lax
from jax.experimental import pallas as pl
from jax.experimental.pallas import tpu as pltpu
from jax.sharding import PartitionSpec as P

STEP = 10
X, Y, C = 2, 4, 2
G = 8
ROWS = 256
LANES = 128
SHARD = G * ROWS * LANES
CHUNKS = ((0, 160, False), (160, 96, False))
GROUPS = ((0,), (1,))
VMEM = 8 * 2**20


def dp_index(x, y, c):
    return (x * Y + y) * C + c


def dp_perm(move):
    return [
        (dp_index(x, y, c), dp_index(*move(x, y, c)))
        for x in range(X)
        for y in range(Y)
        for c in range(C)
    ]


CORE_SWAP = dp_perm(lambda x, y, c: (x, y, 1 - c))
X_SWAP = dp_perm(lambda x, y, c: (1 - x, y, c))
Y_ON = dp_perm(lambda x, y, c: (x, (y + (1 if c == 0 else -1)) % Y, c))
Y_BACK = dp_perm(lambda x, y, c: (x, (y - (1 if c == 0 else -1)) % Y, c))


SHARE = 4096


def params():
    return pltpu.CompilerParams(vmem_limit_bytes=VMEM)


def block_table(x, y, of_core, x_first):
    way = 1 - 2 * of_core
    ys = [(y + step) % Y for step in (2, -way, way, 0)]
    if x_first:
        return [dp_index(at, to, of_core) for at in (1 - x, x) for to in ys]
    return [dp_index(at, to, of_core) for to in ys for at in (x, 1 - x)]


TABLES = np.array(
    [
        sum((block_table(x, y, of, f) for of in (1 - c, c) for f in (False, True)), [])
        for x in range(X)
        for y in range(Y)
        for c in range(C)
    ],
    np.int32,
)


def cost(size):
    return pl.CostEstimate(flops=0, transcendentals=0, bytes_accessed=size // SHARE)


def in_hbm(value):
    return pltpu.with_memory_space_constraint(value, pltpu.HBM)


def in_vmem(value):
    return pltpu.with_memory_space_constraint(value, pltpu.VMEM)


def after(value, *others):
    return lax.optimization_barrier((value, *others))[0]


def combine_kernel(tasks, table, grad, *refs):
    arrays = sum(len(term["rows"]) for task in tasks for term in task["terms"])
    pieces = sum(len(task["splits"]) for task in tasks)
    given, outs, scratch = refs[:arrays], refs[arrays : arrays + pieces], refs[arrays + pieces :]
    work = []
    for task in tasks:
        (held, sems), scratch = scratch[:2], scratch[2:]
        count, size = sum(task["splits"]), task["rows"] * LANES
        copies = [
            [
                pltpu.make_async_copy(
                    grad.at[
                        pl.ds(pl.multiple_of(table[task["first"] + i] * G, G), G),
                        :,
                        pl.ds(task["start"] * LANES, size),
                    ],
                    held.at[pl.ds(i * G, G)],
                    sems.at[i],
                )
            ]
            for i in range(count)
        ]
        terms = []
        for term in task["terms"]:
            mine, given = given[: len(term["rows"])], given[len(term["rows"]) :]
            blocks = [i for i in range(count) if 0 <= term["offset"] + i < mine[0].shape[0]]
            if task["far"]:
                (near, near_sems), scratch = scratch[:2], scratch[2:]
                for i in blocks:
                    copy = pltpu.make_async_copy(
                        mine[0].at[term["offset"] + i], near.at[i], near_sems.at[i]
                    )
                    copies[i].append(copy)
                terms.append({i: ((near, i),) for i in blocks})
            else:
                terms.append({i: tuple((a, term["offset"] + i) for a in mine) for i in blocks})
        for block in copies:
            for copy in block:
                copy.start()
        work.append((held, copies, terms))
    for task, (held, copies, terms) in zip(tasks, work):
        places = [(out, i) for out, n in zip(outs, task["splits"]) for i in range(n)]
        outs = outs[len(task["splits"]) :]
        for i, (block, (out, at)) in enumerate(zip(copies, places)):
            for copy in block:
                copy.wait()
            for j in range(G):
                total = held[i * G + j].reshape(task["rows"], LANES).astype(jnp.float32)
                for term in terms:
                    if i in term:
                        parts = [a[b, j] for a, b in term[i]]
                        total = total + (parts[0] if len(parts) == 1 else jnp.concatenate(parts))
                out[at, j] = total


def combine(grad, table, tasks, name):
    arrays, places, static, scratch = [], [], [], []
    for task in tasks:
        count, rows = sum(task["splits"]), task["rows"]
        scratch.append(pltpu.VMEM((count * G, 1, rows * LANES), jnp.bfloat16))
        scratch.append(pltpu.SemaphoreType.DMA((count,)))
        for held, _ in task["terms"]:
            for a in held:
                arrays.append(in_hbm(a) if task["far"] else in_vmem(a))
                places.append(pl.BlockSpec(memory_space=pl.ANY if task["far"] else pltpu.VMEM))
            if task["far"]:
                scratch.append(pltpu.VMEM((count, G, rows, LANES), jnp.float32))
                scratch.append(pltpu.SemaphoreType.DMA((count,)))
        terms = [dict(rows=[a.shape[2] for a in held], offset=o) for held, o in task["terms"]]
        static.append({**task, "terms": terms})
    shapes = [(n, task["rows"]) for task in tasks for n in task["splits"]]
    size = sum(n * G * rows * LANES * 8 for n, rows in shapes) + sum(a.size * 4 for a in arrays)
    outs = pl.pallas_call(
        functools.partial(combine_kernel, static),
        grid_spec=pltpu.PrefetchScalarGridSpec(
            num_scalar_prefetch=1,
            grid=(),
            in_specs=[pl.BlockSpec(memory_space=pl.ANY)] + places,
            out_specs=[pl.BlockSpec(memory_space=pltpu.VMEM)] * len(shapes),
            scratch_shapes=scratch,
        ),
        out_shape=[pltpu.VMEM((n, G, rows, LANES), jnp.float32) for n, rows in shapes],
        name=name,
        compiler_params=params(),
        cost_estimate=cost(size),
    )(table, in_hbm(grad), *arrays)
    results = []
    for task in tasks:
        results.append(outs[: len(task["splits"])])
        outs = outs[len(task["splits"]) :]
    return results


def order_kernel(holder, *refs):
    (*state, ordered), sems = refs[:-1], refs[-1]
    copies = [
        pltpu.make_async_copy(state[s].at[j], ordered.at[holder[j], s], sems.at[j, s])
        for j in range(G)
        for s in range(3)
    ]
    for copy in copies:
        copy.start()
    for copy in copies:
        copy.wait()


def order_state(state, holder):
    return pl.pallas_call(
        order_kernel,
        grid_spec=pltpu.PrefetchScalarGridSpec(
            num_scalar_prefetch=1,
            grid=(),
            in_specs=[pl.BlockSpec(memory_space=pltpu.VMEM)] * 3,
            out_specs=pl.BlockSpec(memory_space=pl.ANY),
            scratch_shapes=[pltpu.SemaphoreType.DMA((G, 3))],
        ),
        out_shape=pltpu.HBM((G, 3, ROWS, LANES), jnp.float32),
        name="order",
        compiler_params=params(),
        cost_estimate=cost(G * 3 * ROWS * LANES * 8),
    )(holder, *[in_vmem(a) for a in state])


def finish_kernel(terms, first, rows, holder, *refs):
    parts = refs[:terms]
    ordered, total, sems = refs[-3:]
    copies = []
    for j in range(G):
        grad = parts[0][0, j]
        for part in parts[1:]:
            grad = grad + part[0, j]
        total[j] = grad
        copy = pltpu.make_async_copy(
            total.at[j], ordered.at[holder[j], pl.ds(first, rows)], sems.at[j]
        )
        copy.start()
        copies.append(copy)
    for copy in copies:
        copy.wait()


def finish(parts, ordered, holder, first, rows, group_rows):
    held = [] if ordered is None else [in_hbm(ordered)]
    return pl.pallas_call(
        functools.partial(finish_kernel, len(parts), first, rows),
        grid_spec=pltpu.PrefetchScalarGridSpec(
            num_scalar_prefetch=1,
            grid=(),
            in_specs=[pl.BlockSpec(memory_space=pltpu.VMEM)] * len(parts)
            + [pl.BlockSpec(memory_space=pl.ANY)] * len(held),
            out_specs=pl.BlockSpec(memory_space=pl.ANY),
            scratch_shapes=[
                pltpu.VMEM((G, rows, LANES), jnp.float32),
                pltpu.SemaphoreType.DMA((G,)),
            ],
        ),
        out_shape=pltpu.HBM((G, group_rows, LANES), jnp.float32),
        name="finish",
        input_output_aliases={1 + len(parts): 0} if held else {},
        compiler_params=params(),
        cost_estimate=cost(G * rows * LANES * 4 * (len(parts) + 2)),
    )(holder, *[in_vmem(a) for a in parts], *held)


def adam_step(grad, old, first, second):
    m = 0.9 * first + 0.1 * grad
    v = 0.95 * second + 0.05 * grad * grad
    first_hat = m / (1.0 - 0.9**STEP)
    second_hat = v / (1.0 - 0.95**STEP)
    w = old - 0.01 * (first_hat / (jnp.sqrt(second_hat) + 1e-08) + 0.1 * old)
    return w, m, v


def adam_kernel(first, rows, start, holder, ordered, *refs):
    state, refs = refs[:3], refs[3:]
    *outs, grads, old, fresh, grad_sems, in_sems, out_sems = refs[-9:]
    here = pl.ds(start, rows)
    half = G // 2
    loads, stores = [[], []], []
    for n in range(2):
        pieces = pl.ds(n * half, half)
        for j in range(n * half, (n + 1) * half):
            source = ordered.at[holder[j], pl.ds(first, rows)]
            loads[n].append(pltpu.make_async_copy(source, grads.at[j], grad_sems.at[j]))
        for s in range(3):
            source = state[s].at[pieces, here]
            loads[n].append(pltpu.make_async_copy(source, old.at[s, pieces], in_sems.at[n, s]))
        for load in loads[n]:
            load.start()
    for n in range(2):
        pieces = pl.ds(n * half, half)
        for load in loads[n]:
            load.wait()
        for j in range(n * half, (n + 1) * half):
            for s, value in enumerate(adam_step(grads[j], *[old[s, j] for s in range(3)])):
                fresh[s, j] = value
        for s in range(3):
            target = outs[s].at[pieces, here]
            stores.append(pltpu.make_async_copy(fresh.at[s, pieces], target, out_sems.at[n, s]))
            stores[-1].start()
    for store in stores:
        store.wait()


def adam(ordered, state, done, holder, first, start, rows):
    held = [in_hbm(a) for a in done or ()]
    return pl.pallas_call(
        functools.partial(adam_kernel, first, rows, start),
        grid_spec=pltpu.PrefetchScalarGridSpec(
            num_scalar_prefetch=1,
            grid=(),
            in_specs=[pl.BlockSpec(memory_space=pl.ANY)] * (4 + len(held)),
            out_specs=[pl.BlockSpec(memory_space=pl.ANY)] * 3,
            scratch_shapes=[
                pltpu.VMEM((G, rows, LANES), jnp.float32),
                pltpu.VMEM((3, G, rows, LANES), jnp.float32),
                pltpu.VMEM((3, G, rows, LANES), jnp.float32),
                pltpu.SemaphoreType.DMA((G,)),
                pltpu.SemaphoreType.DMA((2, 3)),
                pltpu.SemaphoreType.DMA((2, 3)),
            ],
        ),
        out_shape=[pltpu.HBM((G, ROWS, LANES), jnp.float32)] * 3,
        name="adam",
        input_output_aliases={5 + n: n for n in range(len(held))},
        compiler_params=params(),
        cost_estimate=cost(G * rows * LANES * 4 * 7),
    )(holder, in_hbm(ordered), *[in_hbm(a) for a in state], *held)


def parity_kernel(start, rows, coeff, sums, old, *refs):
    out, near_sums, near_old, fresh, in_sems, out_sems = refs[-6:]
    size = rows // 2
    loads, stores = [], []
    for n in range(2):
        mine, whole = pl.ds(n * size, size), pl.ds(start + n * size, size)
        loads.append(
            [
                pltpu.make_async_copy(sums.at[:, mine], near_sums.at[:, mine], in_sems.at[n, 0]),
                pltpu.make_async_copy(
                    old.at[:, :, whole], near_old.at[:, :, mine], in_sems.at[n, 1]
                ),
            ]
        )
        for load in loads[n]:
            load.start()
    for n in range(2):
        mine, whole = pl.ds(n * size, size), pl.ds(start + n * size, size)
        for load in loads[n]:
            load.wait()
        totals = [[None] * 2 for _ in range(3)]
        for g in range(G):
            values = adam_step(near_sums[g, mine], *[near_old[g, s, mine] for s in range(3)])
            for s, value in enumerate(values):
                for k in range(2):
                    term = coeff[k, g] * value
                    totals[s][k] = term if g == 0 else totals[s][k] + term
        for s in range(3):
            for k in range(2):
                fresh[s, mine, k, :] = totals[s][k]
        stores.append(pltpu.make_async_copy(fresh.at[:, mine], out.at[:, whole], out_sems.at[n]))
        stores[n].start()
    for store in stores:
        store.wait()


def parity(sums, old, coeff, done, start, rows):
    held = [] if done is None else [in_hbm(done)]
    return pl.pallas_call(
        functools.partial(parity_kernel, start, rows),
        grid_spec=pltpu.PrefetchScalarGridSpec(
            num_scalar_prefetch=1,
            grid=(),
            in_specs=[pl.BlockSpec(memory_space=pl.ANY)] * (2 + len(held)),
            out_specs=pl.BlockSpec(memory_space=pl.ANY),
            scratch_shapes=[
                pltpu.VMEM((G, rows, LANES), jnp.float32),
                pltpu.VMEM((G, 3, rows, LANES), jnp.float32),
                pltpu.VMEM((3, rows, 2, LANES), jnp.float32),
                pltpu.SemaphoreType.DMA((2, 2)),
                pltpu.SemaphoreType.DMA((2,)),
            ],
        ),
        out_shape=pltpu.HBM((3, ROWS, 2, LANES), jnp.float32),
        name="parity",
        input_output_aliases={3: 0} if held else {},
        compiler_params=params(),
        cost_estimate=cost(G * 4 * rows * LANES * 4),
    )(coeff, sums, old, *held)


def per_device(
    grad_parts, master_weights, first_moment, second_moment, cauchy_points, parity_holder
):
    index = lax.axis_index("dp")
    holder = parity_holder.reshape(G)
    state = [a.reshape(G, ROWS, LANES) for a in (master_weights, first_moment, second_moment)]
    points = cauchy_points.astype(jnp.float32)
    coeff = 1.0 / (points[:2][:, None] + points[2:][None, :])

    grad = grad_parts.reshape(X * Y * C * G, 1, ROWS * LANES)
    blocks = lax.dynamic_index_in_dim(jnp.asarray(TABLES), index, keepdims=False)
    half = X * Y // 2
    got, across, hop, totals, ordered, sums = {}, {}, {}, {}, {}, {}
    olds, done, shards, token = None, None, None, ()

    def task(n, own, first, splits, terms, part=None, far=False):
        start, rows, x_first = CHUNKS[n]
        if part:
            start, rows = start + part[0], part[1]
        base = X * Y * (2 * own + x_first)
        return dict(first=base + first, start=start, rows=rows, splits=splits, terms=terms, far=far)

    def send(value, name, n, pairs):
        with jax.named_scope(f"{name}_{n}"):
            return lax.ppermute(value, "dp", pairs)

    def run(*jobs, wait=()):
        nonlocal token
        table = after(blocks, *token, *wait)
        name = "_".join(f"{job[2]}{job[3]}" for job in jobs)
        results = combine(grad, table, [job[0] for job in jobs], name)
        token = (results[0][0],)
        for (_, use, *_), result in zip(jobs, results):
            use(*result)

    def then(*values):
        nonlocal token
        token = values

    def swap_core(n, first, splits, part=None):
        def use(*sent):
            at = first
            for a in sent:
                got.setdefault((n, part), []).append((at, send(a, "core", n, CORE_SWAP)))
                at += a.shape[0]

        return task(n, False, first, splits, [], part), use, "core", n

    def terms_at(n, first, count, part=None):
        held = got[n, part] + (across[n] if CHUNKS[n][2] else [])
        return [((a,), first - at) for at, a in held if first < at + a.shape[0] and at < first + count]

    def x_sum(n):
        def use(*sent):
            across[n] = [(half + 2 * i, send(a, "cross", n, X_SWAP)) for i, a in enumerate(sent)]

        terms = [((a,), -at) for at, a in got[n, None] if at < half]
        return task(n, True, 0, (2, 2), terms), use, "cross", n

    def far(n, part=None):
        first, size = (half, 1) if CHUNKS[n][2] else (0, X)

        def use(block):
            hop[n, 0] = hop.get((n, 0), ()) + (send(block, "far", n, Y_ON),)

        return task(n, True, first, (size,), terms_at(n, first, size, part), part), use, "far", n

    def near(n):
        first, size = (half + 1, 1) if CHUNKS[n][2] else (X, X)

        def use(block):
            hop[n, 1] = (send(block, "near", n, Y_BACK),)

        return task(n, True, first, (size,), terms_at(n, first, size)), use, "near", n

    def ahead(n):
        first, size = (half + 2, 1) if CHUNKS[n][2] else (half, X)

        def use(block):
            hop[n, 2] = (send(block, "ahead", n, Y_ON),)

        terms = terms_at(n, first, size) + [(hop[n, 0], 0)]
        return task(n, True, first, (size,), terms), use, "ahead", n

    def here(n, from_hbm=False):
        first, splits = (half + 3, (1,)) if CHUNKS[n][2] else (half + X, (1, 1))

        def use(own, *block):
            totals[n] = [own] + [send(b, "swap", n, X_SWAP) for b in block]

        terms = terms_at(n, first, len(splits)) + [(hop[n, 2], 0), (hop[n, 1], 0)]
        return task(n, True, first, splits, terms, far=from_hbm), use, "here", n

    def place(n):
        (group,) = [g for g in GROUPS if n in g]
        base = min(CHUNKS[m][0] for m in group)
        return group, CHUNKS[n][0] - base, sum(CHUNKS[m][1] for m in group)

    def give(n):
        group, first, group_rows = place(n)
        rows = CHUNKS[n][1]
        parts, before = totals[n], ordered.get(group)
        ordered[group] = finish(parts, before, after(holder, *token), first, rows, group_rows)
        then(ordered[group])

    def to_holders(group):
        sums[group] = lax.all_to_all(ordered[group], "group", 0, 0)

    def update(n):
        nonlocal done
        group, first, _ = place(n)
        start, rows, _ = CHUNKS[n]
        done = adam(ordered[group], state, done, after(holder, *token), first, start, rows)
        then(done[0])

    def parities(group):
        nonlocal shards
        start = min(CHUNKS[m][0] for m in group)
        rows = sum(CHUNKS[m][1] for m in group)
        shards = parity(sums[group], olds, after(coeff, *token), shards, start, rows)
        then(shards)

    run(swap_core(0, 0, (1, 1)))
    run(swap_core(0, 2, (1, 1)))
    run(far(0))
    old = order_state(state, after(holder, *token))
    then(old)
    olds = lax.all_to_all(old, 'group', 0, 0)
    run(near(0), swap_core(0, 4, (1, 1, 1, 1)))
    run(swap_core(1, 0, (1, 1, 1, 1)), swap_core(1, 4, (1, 1, 1, 1)))
    run(ahead(0))
    run(far(1), wait=hop[0, 1])
    run(near(1))
    run(here(0))
    run(ahead(1))
    give(0)
    to_holders((0,))
    run(here(1, True))
    update(0)
    give(1)
    to_holders((1,))
    parities((0,))
    update(1)
    parities((1,))
    outs = [a.reshape(1, SHARD) for a in done]
    return (*outs, shards.transpose(2, 0, 1, 3).reshape(1, 1, 2, 3, ROWS * LANES))


def solution(mesh):
    in_specs = (
        P("dp", "group", None),
        P("group", "dp"),
        P("group", "dp"),
        P("group", "dp"),
        P(),
        P("dp", None),
    )
    out_specs = (
        P("group", "dp"),
        P("group", "dp"),
        P("group", "dp"),
        P("dp", "group", None, None, None),
    )
    return jax.shard_map(
        per_device, mesh=mesh, in_specs=in_specs, out_specs=out_specs, check_vma=False
    )
```

```python
import functools

import jax
import jax.numpy as jnp
import numpy as np
from jax import lax
from jax.experimental import pallas as pl
from jax.experimental.pallas import tpu as pltpu
from jax.sharding import PartitionSpec as P

STEP = 10
X, Y, C = 2, 4, 2
G = 8
ROWS = 256
LANES = 128
SHARD = G * ROWS * LANES
CHUNKS = ((0, 160, False), (160, 96, False))
GROUPS = ((0,), (1,))
VMEM = 8 * 2**20


def dp_index(x, y, c):
    return (x * Y + y) * C + c


def dp_perm(move):
    return [
        (dp_index(x, y, c), dp_index(*move(x, y, c)))
        for x in range(X)
        for y in range(Y)
        for c in range(C)
    ]


CORE_SWAP = dp_perm(lambda x, y, c: (x, y, 1 - c))
X_SWAP = dp_perm(lambda x, y, c: (1 - x, y, c))
Y_ON = dp_perm(lambda x, y, c: (x, (y + (1 if c == 0 else -1)) % Y, c))
Y_BACK = dp_perm(lambda x, y, c: (x, (y - (1 if c == 0 else -1)) % Y, c))


SHARE = 4096


def params():
    return pltpu.CompilerParams(vmem_limit_bytes=VMEM)


def cost(size):
    return pl.CostEstimate(flops=0, transcendentals=0, bytes_accessed=size // SHARE)


def in_hbm(value):
    return pltpu.with_memory_space_constraint(value, pltpu.HBM)


def in_vmem(value):
    return pltpu.with_memory_space_constraint(value, pltpu.VMEM)


def after(value, *others):
    return lax.optimization_barrier((value, *others))[0]


def block_at(place, own):
    index = lax.axis_index("dp")
    core, y, x = lax.rem(index, C), lax.rem(lax.div(index, C), Y), lax.div(index, C * Y)
    of_core = core if own else 1 - core
    way = 1 - 2 * of_core
    to = lax.rem(y + (2, Y - way, Y + way, 0)[place // X], Y)
    at = x if place % X == 0 else 1 - x
    return (at * Y + to) * C + of_core


def combine_kernel(tasks, order, grad, *refs):
    del order
    arrays = sum(len(term["rows"]) for task in tasks for term in task["terms"])
    pieces = sum(len(task["splits"]) for task in tasks)
    given, outs, scratch = refs[:arrays], refs[arrays : arrays + pieces], refs[arrays + pieces :]
    work = []
    for task in tasks:
        (held, sems), scratch = scratch[:2], scratch[2:]
        count, size = sum(task["splits"]), task["rows"] * LANES
        copies = [
            [
                pltpu.make_async_copy(
                    grad.at[
                        pl.ds(pl.multiple_of(block_at(task["first"] + i, task["own"]) * G, G), G),
                        :,
                        pl.ds(task["start"] * LANES, size),
                    ],
                    held.at[pl.ds(i * G, G)],
                    sems.at[i],
                )
            ]
            for i in range(count)
        ]
        terms = []
        for term in task["terms"]:
            mine, given = given[: len(term["rows"])], given[len(term["rows"]) :]
            blocks = [i for i in range(count) if 0 <= term["offset"] + i < mine[0].shape[0]]
            if task["far"]:
                (near, near_sems), scratch = scratch[:2], scratch[2:]
                for i in blocks:
                    copy = pltpu.make_async_copy(
                        mine[0].at[term["offset"] + i], near.at[i], near_sems.at[i]
                    )
                    copies[i].append(copy)
                terms.append({i: ((near, i),) for i in blocks})
            else:
                terms.append({i: tuple((a, term["offset"] + i) for a in mine) for i in blocks})
        for block in copies:
            for copy in block:
                copy.start()
        work.append((held, copies, terms))
    for task, (held, copies, terms) in zip(tasks, work):
        places = [(out, i) for out, n in zip(outs, task["splits"]) for i in range(n)]
        outs = outs[len(task["splits"]) :]
        for i, (block, (out, at)) in enumerate(zip(copies, places)):
            for copy in block:
                copy.wait()
            for j in range(G):
                total = held[i * G + j].reshape(task["rows"], LANES).astype(jnp.float32)
                for term in terms:
                    if i in term:
                        parts = [a[b, j] for a, b in term[i]]
                        total = total + (parts[0] if len(parts) == 1 else jnp.concatenate(parts))
                out[at, j] = total


def combine(grad, order, tasks, name):
    arrays, places, static, scratch = [], [], [], []
    for task in tasks:
        count, rows = sum(task["splits"]), task["rows"]
        scratch.append(pltpu.VMEM((count * G, 1, rows * LANES), jnp.bfloat16))
        scratch.append(pltpu.SemaphoreType.DMA((count,)))
        for held, _ in task["terms"]:
            for a in held:
                arrays.append(in_hbm(a) if task["far"] else in_vmem(a))
                places.append(pl.BlockSpec(memory_space=pl.ANY if task["far"] else pltpu.VMEM))
            if task["far"]:
                scratch.append(pltpu.VMEM((count, G, rows, LANES), jnp.float32))
                scratch.append(pltpu.SemaphoreType.DMA((count,)))
        terms = [dict(rows=[a.shape[2] for a in held], offset=o) for held, o in task["terms"]]
        static.append({**task, "terms": terms})
    shapes = [(n, task["rows"]) for task in tasks for n in task["splits"]]
    size = sum(n * G * rows * LANES * 8 for n, rows in shapes) + sum(a.size * 4 for a in arrays)
    outs = pl.pallas_call(
        functools.partial(combine_kernel, static),
        grid_spec=pltpu.PrefetchScalarGridSpec(
            num_scalar_prefetch=0,
            grid=(),
            in_specs=[pl.BlockSpec(memory_space=pl.ANY)] * 2 + places,
            out_specs=[pl.BlockSpec(memory_space=pltpu.VMEM)] * len(shapes),
            scratch_shapes=scratch,
        ),
        out_shape=[pltpu.VMEM((n, G, rows, LANES), jnp.float32) for n, rows in shapes],
        name=name,
        compiler_params=params(),
        cost_estimate=cost(size),
    )(order, in_hbm(grad), *arrays)
    results = []
    for task in tasks:
        results.append(outs[: len(task["splits"])])
        outs = outs[len(task["splits"]) :]
    return results


def order_kernel(holder, *refs):
    (*state, ordered), sems = refs[:-1], refs[-1]
    copies = [
        pltpu.make_async_copy(state[s].at[j], ordered.at[holder[j], s], sems.at[j, s])
        for j in range(G)
        for s in range(3)
    ]
    for copy in copies:
        copy.start()
    for copy in copies:
        copy.wait()


def order_state(state, holder):
    return pl.pallas_call(
        order_kernel,
        grid_spec=pltpu.PrefetchScalarGridSpec(
            num_scalar_prefetch=1,
            grid=(),
            in_specs=[pl.BlockSpec(memory_space=pltpu.VMEM)] * 3,
            out_specs=pl.BlockSpec(memory_space=pl.ANY),
            scratch_shapes=[pltpu.SemaphoreType.DMA((G, 3))],
        ),
        out_shape=pltpu.HBM((G, 3, ROWS, LANES), jnp.float32),
        name="order",
        compiler_params=params(),
        cost_estimate=cost(G * 3 * ROWS * LANES * 8),
    )(holder, *[in_vmem(a) for a in state])


def finish_kernel(terms, first, rows, holder, *refs):
    parts = refs[:terms]
    ordered, total, sems = refs[-3:]
    copies = []
    for j in range(G):
        grad = parts[0][0, j]
        for part in parts[1:]:
            grad = grad + part[0, j]
        total[j] = grad
        copy = pltpu.make_async_copy(
            total.at[j], ordered.at[holder[j], pl.ds(first, rows)], sems.at[j]
        )
        copy.start()
        copies.append(copy)
    for copy in copies:
        copy.wait()


def finish(parts, ordered, holder, first, rows, group_rows):
    held = [] if ordered is None else [in_hbm(ordered)]
    return pl.pallas_call(
        functools.partial(finish_kernel, len(parts), first, rows),
        grid_spec=pltpu.PrefetchScalarGridSpec(
            num_scalar_prefetch=1,
            grid=(),
            in_specs=[pl.BlockSpec(memory_space=pltpu.VMEM)] * len(parts)
            + [pl.BlockSpec(memory_space=pl.ANY)] * len(held),
            out_specs=pl.BlockSpec(memory_space=pl.ANY),
            scratch_shapes=[
                pltpu.VMEM((G, rows, LANES), jnp.float32),
                pltpu.SemaphoreType.DMA((G,)),
            ],
        ),
        out_shape=pltpu.HBM((G, group_rows, LANES), jnp.float32),
        name="finish",
        input_output_aliases={1 + len(parts): 0} if held else {},
        compiler_params=params(),
        cost_estimate=cost(G * rows * LANES * 4 * (len(parts) + 2)),
    )(holder, *[in_vmem(a) for a in parts], *held)


def adam_step(grad, old, first, second):
    m = 0.9 * first + 0.1 * grad
    v = 0.95 * second + 0.05 * grad * grad
    first_hat = m / (1.0 - 0.9**STEP)
    second_hat = v / (1.0 - 0.95**STEP)
    w = old - 0.01 * (first_hat / (jnp.sqrt(second_hat) + 1e-08) + 0.1 * old)
    return w, m, v


def adam_kernel(first, rows, start, holder, ordered, *refs):
    state, refs = refs[:3], refs[3:]
    *outs, grads, old, fresh, grad_sems, in_sems, out_sems = refs[-9:]
    here = pl.ds(start, rows)
    half = G // 2
    loads, stores = [[], []], []
    for n in range(2):
        pieces = pl.ds(n * half, half)
        for j in range(n * half, (n + 1) * half):
            source = ordered.at[holder[j], pl.ds(first, rows)]
            loads[n].append(pltpu.make_async_copy(source, grads.at[j], grad_sems.at[j]))
        for s in range(3):
            source = state[s].at[pieces, here]
            loads[n].append(pltpu.make_async_copy(source, old.at[s, pieces], in_sems.at[n, s]))
        for load in loads[n]:
            load.start()
    for n in range(2):
        pieces = pl.ds(n * half, half)
        for load in loads[n]:
            load.wait()
        for j in range(n * half, (n + 1) * half):
            for s, value in enumerate(adam_step(grads[j], *[old[s, j] for s in range(3)])):
                fresh[s, j] = value
        for s in range(3):
            target = outs[s].at[pieces, here]
            stores.append(pltpu.make_async_copy(fresh.at[s, pieces], target, out_sems.at[n, s]))
            stores[-1].start()
    for store in stores:
        store.wait()


def adam(ordered, state, done, holder, first, start, rows):
    held = [in_hbm(a) for a in done or ()]
    return pl.pallas_call(
        functools.partial(adam_kernel, first, rows, start),
        grid_spec=pltpu.PrefetchScalarGridSpec(
            num_scalar_prefetch=1,
            grid=(),
            in_specs=[pl.BlockSpec(memory_space=pl.ANY)] * (4 + len(held)),
            out_specs=[pl.BlockSpec(memory_space=pl.ANY)] * 3,
            scratch_shapes=[
                pltpu.VMEM((G, rows, LANES), jnp.float32),
                pltpu.VMEM((3, G, rows, LANES), jnp.float32),
                pltpu.VMEM((3, G, rows, LANES), jnp.float32),
                pltpu.SemaphoreType.DMA((G,)),
                pltpu.SemaphoreType.DMA((2, 3)),
                pltpu.SemaphoreType.DMA((2, 3)),
            ],
        ),
        out_shape=[pltpu.HBM((G, ROWS, LANES), jnp.float32)] * 3,
        name="adam",
        input_output_aliases={5 + n: n for n in range(len(held))},
        compiler_params=params(),
        cost_estimate=cost(G * rows * LANES * 4 * 7),
    )(holder, in_hbm(ordered), *[in_hbm(a) for a in state], *held)


def parity_kernel(start, rows, coeff, sums, old, *refs):
    out, near_sums, near_old, fresh, in_sems, out_sems = refs[-6:]
    size = rows // 2
    loads, stores = [], []
    for n in range(2):
        mine, whole = pl.ds(n * size, size), pl.ds(start + n * size, size)
        loads.append(
            [
                pltpu.make_async_copy(sums.at[:, mine], near_sums.at[:, mine], in_sems.at[n, 0]),
                pltpu.make_async_copy(
                    old.at[:, :, whole], near_old.at[:, :, mine], in_sems.at[n, 1]
                ),
            ]
        )
        for load in loads[n]:
            load.start()
    for n in range(2):
        mine, whole = pl.ds(n * size, size), pl.ds(start + n * size, size)
        for load in loads[n]:
            load.wait()
        totals = [[None] * 2 for _ in range(3)]
        for g in range(G):
            values = adam_step(near_sums[g, mine], *[near_old[g, s, mine] for s in range(3)])
            for s, value in enumerate(values):
                for k in range(2):
                    term = coeff[k, g] * value
                    totals[s][k] = term if g == 0 else totals[s][k] + term
        for s in range(3):
            for k in range(2):
                fresh[s, mine, k, :] = totals[s][k]
        stores.append(pltpu.make_async_copy(fresh.at[:, mine], out.at[:, whole], out_sems.at[n]))
        stores[n].start()
    for store in stores:
        store.wait()


def parity(sums, old, coeff, done, start, rows):
    held = [] if done is None else [in_hbm(done)]
    return pl.pallas_call(
        functools.partial(parity_kernel, start, rows),
        grid_spec=pltpu.PrefetchScalarGridSpec(
            num_scalar_prefetch=1,
            grid=(),
            in_specs=[pl.BlockSpec(memory_space=pl.ANY)] * (2 + len(held)),
            out_specs=pl.BlockSpec(memory_space=pl.ANY),
            scratch_shapes=[
                pltpu.VMEM((G, rows, LANES), jnp.float32),
                pltpu.VMEM((G, 3, rows, LANES), jnp.float32),
                pltpu.VMEM((3, rows, 2, LANES), jnp.float32),
                pltpu.SemaphoreType.DMA((2, 2)),
                pltpu.SemaphoreType.DMA((2,)),
            ],
        ),
        out_shape=pltpu.HBM((3, ROWS, 2, LANES), jnp.float32),
        name="parity",
        input_output_aliases={3: 0} if held else {},
        compiler_params=params(),
        cost_estimate=cost(G * 4 * rows * LANES * 4),
    )(coeff, sums, old, *held)


def per_device(
    grad_parts, master_weights, first_moment, second_moment, cauchy_points, parity_holder
):
    holder = parity_holder.reshape(G)
    state = [a.reshape(G, ROWS, LANES) for a in (master_weights, first_moment, second_moment)]
    points = cauchy_points.astype(jnp.float32)
    coeff = 1.0 / (points[:2][:, None] + points[2:][None, :])

    grad = grad_parts.reshape(X * Y * C * G, 1, ROWS * LANES)
    blocks = jnp.zeros((1,), jnp.int32)
    half = X * Y // 2
    got, across, hop, totals, ordered, sums = {}, {}, {}, {}, {}, {}
    olds, done, shards, token = None, None, None, ()

    def task(n, own, first, splits, terms, part=None, far=False):
        start, rows, _ = CHUNKS[n]
        if part:
            start, rows = start + part[0], part[1]
        return dict(own=own, first=first, start=start, rows=rows, splits=splits, terms=terms, far=far)

    def send(value, name, n, pairs):
        with jax.named_scope(f"{name}_{n}"):
            return lax.ppermute(value, "dp", pairs)

    def run(*jobs, wait=()):
        nonlocal token
        order = after(blocks, *token, *wait)
        name = "_".join(f"{job[2]}{job[3]}" for job in jobs)
        results = combine(grad, order, [job[0] for job in jobs], name)
        token = (results[0][0],)
        for (_, use, *_), result in zip(jobs, results):
            use(*result)

    def then(*values):
        nonlocal token
        token = values

    def swap_core(n, first, splits, part=None):
        def use(*sent):
            at = first
            for a in sent:
                got.setdefault((n, part), []).append((at, send(a, "core", n, CORE_SWAP)))
                at += a.shape[0]

        return task(n, False, first, splits, [], part), use, "core", n

    def terms_at(n, first, count, part=None):
        held = got[n, part] + (across[n] if CHUNKS[n][2] else [])
        return [((a,), first - at) for at, a in held if first < at + a.shape[0] and at < first + count]

    def x_sum(n):
        def use(*sent):
            across[n] = [(half + 2 * i, send(a, "cross", n, X_SWAP)) for i, a in enumerate(sent)]

        terms = [((a,), -at) for at, a in got[n, None] if at < half]
        return task(n, True, 0, (2, 2), terms), use, "cross", n

    def far(n, part=None):
        first, size = (half, 1) if CHUNKS[n][2] else (0, X)

        def use(block):
            hop[n, 0] = hop.get((n, 0), ()) + (send(block, "far", n, Y_ON),)

        return task(n, True, first, (size,), terms_at(n, first, size, part), part), use, "far", n

    def near(n):
        first, size = (half + 1, 1) if CHUNKS[n][2] else (X, X)

        def use(block):
            hop[n, 1] = (send(block, "near", n, Y_BACK),)

        return task(n, True, first, (size,), terms_at(n, first, size)), use, "near", n

    def ahead(n):
        first, size = (half + 2, 1) if CHUNKS[n][2] else (half, X)

        def use(block):
            hop[n, 2] = (send(block, "ahead", n, Y_ON),)

        terms = terms_at(n, first, size) + [(hop[n, 0], 0)]
        return task(n, True, first, (size,), terms), use, "ahead", n

    def here(n, from_hbm=False):
        first, splits = (half + 3, (1,)) if CHUNKS[n][2] else (half + X, (1, 1))

        def use(own, *block):
            totals[n] = [own] + [send(b, "swap", n, X_SWAP) for b in block]

        terms = terms_at(n, first, len(splits)) + [(hop[n, 2], 0), (hop[n, 1], 0)]
        return task(n, True, first, splits, terms, far=from_hbm), use, "here", n

    def place(n):
        (group,) = [g for g in GROUPS if n in g]
        base = min(CHUNKS[m][0] for m in group)
        return group, CHUNKS[n][0] - base, sum(CHUNKS[m][1] for m in group)

    def give(n):
        group, first, group_rows = place(n)
        rows = CHUNKS[n][1]
        parts, before = totals[n], ordered.get(group)
        ordered[group] = finish(parts, before, after(holder, *token), first, rows, group_rows)
        then(ordered[group])

    def to_holders(group):
        sums[group] = lax.all_to_all(ordered[group], "group", 0, 0)

    def update(n):
        nonlocal done
        group, first, _ = place(n)
        start, rows, _ = CHUNKS[n]
        done = adam(ordered[group], state, done, after(holder, *token), first, start, rows)
        then(done[0])

    def parities(group):
        nonlocal shards
        start = min(CHUNKS[m][0] for m in group)
        rows = sum(CHUNKS[m][1] for m in group)
        shards = parity(sums[group], olds, after(coeff, *token), shards, start, rows)
        then(shards)

    run(swap_core(0, 0, (1, 1)))
    run(swap_core(0, 2, (1, 1)))
    run(far(0))
    old = order_state(state, after(holder, *token))
    then(old)
    olds = lax.all_to_all(old, 'group', 0, 0)
    run(near(0), swap_core(0, 4, (1, 1, 1, 1)))
    run(swap_core(1, 0, (1, 1, 1, 1)), swap_core(1, 4, (1, 1, 1, 1)))
    run(ahead(0))
    run(far(1), wait=hop[0, 1])
    run(near(1))
    run(here(0))
    run(ahead(1))
    give(0)
    to_holders((0,))
    run(here(1, True))
    update(0)
    give(1)
    to_holders((1,))
    parities((0,))
    update(1)
    parities((1,))
    outs = [a.reshape(1, SHARD) for a in done]
    return (*outs, shards.transpose(2, 0, 1, 3).reshape(1, 1, 2, 3, ROWS * LANES))


def solution(mesh):
    in_specs = (
        P("dp", "group", None),
        P("group", "dp"),
        P("group", "dp"),
        P("group", "dp"),
        P(),
        P("dp", None),
    )
    out_specs = (
        P("group", "dp"),
        P("group", "dp"),
        P("group", "dp"),
        P("dp", "group", None, None, None),
    )
    return jax.shard_map(
        per_device, mesh=mesh, in_specs=in_specs, out_specs=out_specs, check_vma=False
    )
```

```python
import functools

import jax
import jax.numpy as jnp
from jax import lax
from jax.experimental import pallas as pl
from jax.experimental.pallas import tpu as pltpu
from jax.sharding import PartitionSpec as P

STEP = 10
X, Y, C = 2, 4, 2
G = 8
ROWS = 256
LANES = 128
SHARD = G * ROWS * LANES
CHUNKS = ((0, 160), (160, 96))
GROUPS = ((0,), (1,))
VMEM = 8 * 2**20


def dp_index(x, y, c):
    return (x * Y + y) * C + c


def dp_perm(move):
    return [
        (dp_index(x, y, c), dp_index(*move(x, y, c)))
        for x in range(X)
        for y in range(Y)
        for c in range(C)
    ]


CORE_SWAP = dp_perm(lambda x, y, c: (x, y, 1 - c))
X_SWAP = dp_perm(lambda x, y, c: (1 - x, y, c))
Y_ON = dp_perm(lambda x, y, c: (x, (y + (1 if c == 0 else -1)) % Y, c))
Y_BACK = dp_perm(lambda x, y, c: (x, (y - (1 if c == 0 else -1)) % Y, c))


SHARE = 4096


def params():
    return pltpu.CompilerParams(vmem_limit_bytes=VMEM)


def cost(size):
    return pl.CostEstimate(flops=0, transcendentals=0, bytes_accessed=size // SHARE)


def in_hbm(value):
    return pltpu.with_memory_space_constraint(value, pltpu.HBM)


def in_vmem(value):
    return pltpu.with_memory_space_constraint(value, pltpu.VMEM)


def after(value, *others):
    return lax.optimization_barrier((value, *others))[0]


def block_at(place, own):
    index = lax.axis_index("dp")
    core, y, x = lax.rem(index, C), lax.rem(lax.div(index, C), Y), lax.div(index, C * Y)
    of_core = core if own else 1 - core
    way = 1 - 2 * of_core
    to = lax.rem(y + (2, Y - way, Y + way, 0)[place // X], Y)
    at = x if place % X == 0 else 1 - x
    return (at * Y + to) * C + of_core


def combine_kernel(tasks, order, grad, *refs):
    del order
    arrays = sum(len(task["offsets"]) for task in tasks)
    pieces = sum(len(task["splits"]) for task in tasks)
    given, outs, scratch = refs[:arrays], refs[arrays : arrays + pieces], refs[arrays + pieces :]
    work = []
    for task in tasks:
        (held, sems), scratch = scratch[:2], scratch[2:]
        count, size = sum(task["splits"]), task["rows"] * LANES
        copies = [
            [
                pltpu.make_async_copy(
                    grad.at[
                        pl.ds(pl.multiple_of(block_at(task["first"] + i, task["own"]) * G, G), G),
                        :,
                        pl.ds(task["start"] * LANES, size),
                    ],
                    held.at[pl.ds(i * G, G)],
                    sems.at[i],
                )
            ]
            for i in range(count)
        ]
        terms = []
        for offset in task["offsets"]:
            mine, given = given[0], given[1:]
            blocks = [i for i in range(count) if 0 <= offset + i < mine.shape[0]]
            if task["far"]:
                (near, near_sems), scratch = scratch[:2], scratch[2:]
                for i in blocks:
                    source = mine.at[offset + i]
                    copies[i].append(pltpu.make_async_copy(source, near.at[i], near_sems.at[i]))
                terms.append({i: (near, i) for i in blocks})
            else:
                terms.append({i: (mine, offset + i) for i in blocks})
        for block in copies:
            for copy in block:
                copy.start()
        work.append((held, copies, terms))
    for task, (held, copies, terms) in zip(tasks, work):
        places = [(out, i) for out, n in zip(outs, task["splits"]) for i in range(n)]
        outs = outs[len(task["splits"]) :]
        for i, (block, (out, at)) in enumerate(zip(copies, places)):
            for copy in block:
                copy.wait()
            for j in range(G):
                total = held[i * G + j].reshape(task["rows"], LANES).astype(jnp.float32)
                for term in terms:
                    if i in term:
                        held_term, place = term[i]
                        total = total + held_term[place, j]
                out[at, j] = total


def combine(grad, order, tasks, name):
    arrays, places, static, scratch = [], [], [], []
    for task in tasks:
        count, rows = sum(task["splits"]), task["rows"]
        scratch.append(pltpu.VMEM((count * G, 1, rows * LANES), jnp.bfloat16))
        scratch.append(pltpu.SemaphoreType.DMA((count,)))
        for held, _ in task["terms"]:
            arrays.append(in_hbm(held) if task["far"] else in_vmem(held))
            places.append(pl.BlockSpec(memory_space=pl.ANY if task["far"] else pltpu.VMEM))
            if task["far"]:
                scratch.append(pltpu.VMEM((count, G, rows, LANES), jnp.float32))
                scratch.append(pltpu.SemaphoreType.DMA((count,)))
        static.append({**task, "offsets": [offset for _, offset in task["terms"]]})
    shapes = [(n, task["rows"]) for task in tasks for n in task["splits"]]
    size = sum(n * G * rows * LANES * 8 for n, rows in shapes) + sum(a.size * 4 for a in arrays)
    outs = pl.pallas_call(
        functools.partial(combine_kernel, static),
        grid_spec=pltpu.PrefetchScalarGridSpec(
            num_scalar_prefetch=0,
            grid=(),
            in_specs=[pl.BlockSpec(memory_space=pl.ANY)] * 2 + places,
            out_specs=[pl.BlockSpec(memory_space=pltpu.VMEM)] * len(shapes),
            scratch_shapes=scratch,
        ),
        out_shape=[pltpu.VMEM((n, G, rows, LANES), jnp.float32) for n, rows in shapes],
        name=name,
        compiler_params=params(),
        cost_estimate=cost(size),
    )(order, in_hbm(grad), *arrays)
    results = []
    for task in tasks:
        results.append(outs[: len(task["splits"])])
        outs = outs[len(task["splits"]) :]
    return results


def order_kernel(holder, *refs):
    (*state, ordered), sems = refs[:-1], refs[-1]
    copies = [
        pltpu.make_async_copy(state[s].at[j], ordered.at[holder[j], s], sems.at[j, s])
        for j in range(G)
        for s in range(3)
    ]
    for copy in copies:
        copy.start()
    for copy in copies:
        copy.wait()


def order_state(state, holder):
    return pl.pallas_call(
        order_kernel,
        grid_spec=pltpu.PrefetchScalarGridSpec(
            num_scalar_prefetch=1,
            grid=(),
            in_specs=[pl.BlockSpec(memory_space=pltpu.VMEM)] * 3,
            out_specs=pl.BlockSpec(memory_space=pl.ANY),
            scratch_shapes=[pltpu.SemaphoreType.DMA((G, 3))],
        ),
        out_shape=pltpu.HBM((G, 3, ROWS, LANES), jnp.float32),
        name="order",
        compiler_params=params(),
        cost_estimate=cost(G * 3 * ROWS * LANES * 8),
    )(holder, *[in_vmem(a) for a in state])


def finish_kernel(terms, first, rows, holder, *refs):
    parts = refs[:terms]
    ordered, total, sems = refs[-3:]
    copies = []
    for j in range(G):
        grad = parts[0][0, j]
        for part in parts[1:]:
            grad = grad + part[0, j]
        total[j] = grad
        copy = pltpu.make_async_copy(
            total.at[j], ordered.at[holder[j], pl.ds(first, rows)], sems.at[j]
        )
        copy.start()
        copies.append(copy)
    for copy in copies:
        copy.wait()


def finish(parts, ordered, holder, first, rows, group_rows):
    held = [] if ordered is None else [in_hbm(ordered)]
    return pl.pallas_call(
        functools.partial(finish_kernel, len(parts), first, rows),
        grid_spec=pltpu.PrefetchScalarGridSpec(
            num_scalar_prefetch=1,
            grid=(),
            in_specs=[pl.BlockSpec(memory_space=pltpu.VMEM)] * len(parts)
            + [pl.BlockSpec(memory_space=pl.ANY)] * len(held),
            out_specs=pl.BlockSpec(memory_space=pl.ANY),
            scratch_shapes=[
                pltpu.VMEM((G, rows, LANES), jnp.float32),
                pltpu.SemaphoreType.DMA((G,)),
            ],
        ),
        out_shape=pltpu.HBM((G, group_rows, LANES), jnp.float32),
        name="finish",
        input_output_aliases={1 + len(parts): 0} if held else {},
        compiler_params=params(),
        cost_estimate=cost(G * rows * LANES * 4 * (len(parts) + 2)),
    )(holder, *[in_vmem(a) for a in parts], *held)


def adam_step(grad, old, first, second):
    m = 0.9 * first + 0.1 * grad
    v = 0.95 * second + 0.05 * grad * grad
    first_hat = m / (1.0 - 0.9**STEP)
    second_hat = v / (1.0 - 0.95**STEP)
    w = old - 0.01 * (first_hat / (jnp.sqrt(second_hat) + 1e-08) + 0.1 * old)
    return w, m, v


def adam_kernel(first, rows, start, holder, ordered, *refs):
    state, refs = refs[:3], refs[3:]
    *outs, grads, old, fresh, grad_sems, in_sems, out_sems = refs[-9:]
    here = pl.ds(start, rows)
    half = G // 2
    loads, stores = [[], []], []
    for n in range(2):
        pieces = pl.ds(n * half, half)
        for j in range(n * half, (n + 1) * half):
            source = ordered.at[holder[j], pl.ds(first, rows)]
            loads[n].append(pltpu.make_async_copy(source, grads.at[j], grad_sems.at[j]))
        for s in range(3):
            source = state[s].at[pieces, here]
            loads[n].append(pltpu.make_async_copy(source, old.at[s, pieces], in_sems.at[n, s]))
        for load in loads[n]:
            load.start()
    for n in range(2):
        pieces = pl.ds(n * half, half)
        for load in loads[n]:
            load.wait()
        for j in range(n * half, (n + 1) * half):
            for s, value in enumerate(adam_step(grads[j], *[old[s, j] for s in range(3)])):
                fresh[s, j] = value
        for s in range(3):
            target = outs[s].at[pieces, here]
            stores.append(pltpu.make_async_copy(fresh.at[s, pieces], target, out_sems.at[n, s]))
            stores[-1].start()
    for store in stores:
        store.wait()


def adam(ordered, state, done, holder, first, start, rows):
    held = [in_hbm(a) for a in done or ()]
    return pl.pallas_call(
        functools.partial(adam_kernel, first, rows, start),
        grid_spec=pltpu.PrefetchScalarGridSpec(
            num_scalar_prefetch=1,
            grid=(),
            in_specs=[pl.BlockSpec(memory_space=pl.ANY)] * (4 + len(held)),
            out_specs=[pl.BlockSpec(memory_space=pl.ANY)] * 3,
            scratch_shapes=[
                pltpu.VMEM((G, rows, LANES), jnp.float32),
                pltpu.VMEM((3, G, rows, LANES), jnp.float32),
                pltpu.VMEM((3, G, rows, LANES), jnp.float32),
                pltpu.SemaphoreType.DMA((G,)),
                pltpu.SemaphoreType.DMA((2, 3)),
                pltpu.SemaphoreType.DMA((2, 3)),
            ],
        ),
        out_shape=[pltpu.HBM((G, ROWS, LANES), jnp.float32)] * 3,
        name="adam",
        input_output_aliases={5 + n: n for n in range(len(held))},
        compiler_params=params(),
        cost_estimate=cost(G * rows * LANES * 4 * 7),
    )(holder, in_hbm(ordered), *[in_hbm(a) for a in state], *held)


def parity_kernel(start, rows, coeff, sums, old, *refs):
    out, near_coeff, near_sums, near_old, fresh, coeff_sem, in_sems, out_sems = refs[-8:]
    size = rows // 2
    loads, stores = [], []
    coeff_load = pltpu.make_async_copy(coeff, near_coeff, coeff_sem)
    coeff_load.start()
    for n in range(2):
        mine, whole = pl.ds(n * size, size), pl.ds(start + n * size, size)
        loads.append(
            [
                pltpu.make_async_copy(sums.at[:, mine], near_sums.at[:, mine], in_sems.at[n, 0]),
                pltpu.make_async_copy(
                    old.at[:, :, whole], near_old.at[:, :, mine], in_sems.at[n, 1]
                ),
            ]
        )
        for load in loads[n]:
            load.start()
    coeff_load.wait()
    for n in range(2):
        mine, whole = pl.ds(n * size, size), pl.ds(start + n * size, size)
        for load in loads[n]:
            load.wait()
        totals = [[None] * 2 for _ in range(3)]
        for g in range(G):
            values = adam_step(near_sums[g, mine], *[near_old[g, s, mine] for s in range(3)])
            for s, value in enumerate(values):
                for k in range(2):
                    term = near_coeff[pl.ds(k * G + g, 1)] * value
                    totals[s][k] = term if g == 0 else totals[s][k] + term
        for s in range(3):
            for k in range(2):
                fresh[s, mine, k, :] = totals[s][k]
        stores.append(pltpu.make_async_copy(fresh.at[:, mine], out.at[:, whole], out_sems.at[n]))
        stores[n].start()
    for store in stores:
        store.wait()


def parity(sums, old, coeff, done, start, rows):
    held = [] if done is None else [in_hbm(done)]
    return pl.pallas_call(
        functools.partial(parity_kernel, start, rows),
        grid_spec=pltpu.PrefetchScalarGridSpec(
            num_scalar_prefetch=0,
            grid=(),
            in_specs=[pl.BlockSpec(memory_space=pl.ANY)] * (3 + len(held)),
            out_specs=pl.BlockSpec(memory_space=pl.ANY),
            scratch_shapes=[
                pltpu.VMEM((2 * G, LANES), jnp.float32),
                pltpu.VMEM((G, rows, LANES), jnp.float32),
                pltpu.VMEM((G, 3, rows, LANES), jnp.float32),
                pltpu.VMEM((3, rows, 2, LANES), jnp.float32),
                pltpu.SemaphoreType.DMA,
                pltpu.SemaphoreType.DMA((2, 2)),
                pltpu.SemaphoreType.DMA((2,)),
            ],
        ),
        out_shape=pltpu.HBM((3, ROWS, 2, LANES), jnp.float32),
        name="parity",
        input_output_aliases={3: 0} if held else {},
        compiler_params=params(),
        cost_estimate=cost(G * 4 * rows * LANES * 4),
    )(coeff, sums, old, *held)


def per_device(
    grad_parts, master_weights, first_moment, second_moment, cauchy_points, parity_holder
):
    holder = parity_holder.reshape(G)
    state = [a.reshape(G, ROWS, LANES) for a in (master_weights, first_moment, second_moment)]
    points = cauchy_points.astype(jnp.float32)
    coeff = 1.0 / (points[:2][:, None] + points[2:][None, :])
    coeff = jnp.broadcast_to(coeff.reshape(2 * G, 1), (2 * G, LANES))
    grad = grad_parts.reshape(X * Y * C * G, 1, ROWS * LANES)
    nothing = jnp.zeros((1,), jnp.int32)
    half = X * Y // 2
    got, hop, totals, ordered, sums = {}, {}, {}, {}, {}
    olds, done, shards, token = None, None, None, ()

    def task(n, own, first, splits, terms, far=False):
        start, rows = CHUNKS[n]
        return dict(own=own, first=first, start=start, rows=rows, splits=splits, terms=terms, far=far)

    def send(value, name, n, pairs):
        with jax.named_scope(f"{name}_{n}"):
            return lax.ppermute(value, "dp", pairs)

    def run(*jobs, wait=()):
        nonlocal token
        order = after(nothing, *token, *wait)
        name = "_".join(f"{job[2]}{job[3]}" for job in jobs)
        results = combine(grad, order, [job[0] for job in jobs], name)
        token = (results[0][0],)
        for (_, use, *_), result in zip(jobs, results):
            use(*result)

    def then(*values):
        nonlocal token
        token = values

    def swap_core(n, first, splits):
        def use(*sent):
            at = first
            for a in sent:
                got.setdefault(n, []).append((at, send(a, "core", n, CORE_SWAP)))
                at += a.shape[0]

        return task(n, False, first, splits, []), use, "core", n

    def terms_at(n, first, count):
        return [(a, first - at) for at, a in got[n] if first < at + a.shape[0] and at < first + count]

    def far(n):
        def use(block):
            hop[n, 0] = send(block, "far", n, Y_ON)

        return task(n, True, 0, (X,), terms_at(n, 0, X)), use, "far", n

    def near(n):
        def use(block):
            hop[n, 1] = send(block, "near", n, Y_BACK)

        return task(n, True, X, (X,), terms_at(n, X, X)), use, "near", n

    def ahead(n):
        def use(block):
            hop[n, 2] = send(block, "ahead", n, Y_ON)

        terms = terms_at(n, half, X) + [(hop[n, 0], 0)]
        return task(n, True, half, (X,), terms), use, "ahead", n

    def here(n, from_hbm=False):
        def use(own, block):
            totals[n] = [own, send(block, "swap", n, X_SWAP)]

        terms = terms_at(n, half + X, X) + [(hop[n, 2], 0), (hop[n, 1], 0)]
        return task(n, True, half + X, (1, 1), terms, far=from_hbm), use, "here", n

    def place(n):
        (group,) = [g for g in GROUPS if n in g]
        base = min(CHUNKS[m][0] for m in group)
        return group, CHUNKS[n][0] - base, sum(CHUNKS[m][1] for m in group)

    def give(n):
        group, first, group_rows = place(n)
        rows = CHUNKS[n][1]
        parts, before = totals[n], ordered.get(group)
        ordered[group] = finish(parts, before, after(holder, *token), first, rows, group_rows)
        then(ordered[group])

    def to_holders(group):
        sums[group] = lax.all_to_all(ordered[group], "group", 0, 0)

    def update(n):
        nonlocal done
        group, first, _ = place(n)
        start, rows = CHUNKS[n]
        done = adam(ordered[group], state, done, after(holder, *token), first, start, rows)
        then(done[0])

    def parities(group):
        nonlocal shards
        start = min(CHUNKS[m][0] for m in group)
        rows = sum(CHUNKS[m][1] for m in group)
        shards = parity(sums[group], olds, after(coeff, *token), shards, start, rows)
        then(shards)

    run(swap_core(0, 0, (1, 1)))
    run(swap_core(0, 2, (1, 1)))
    run(far(0))
    old = order_state(state, after(holder, *token))
    then(old)
    olds = lax.all_to_all(old, 'group', 0, 0)
    run(near(0), swap_core(0, 4, (1, 1, 1, 1)))
    run(swap_core(1, 0, (1, 1, 1, 1)), swap_core(1, 4, (1, 1, 1, 1)))
    run(ahead(0))
    run(far(1), wait=(hop[0, 1],))
    run(near(1))
    run(here(0))
    run(ahead(1))
    give(0)
    to_holders((0,))
    run(here(1, True))
    update(0)
    give(1)
    to_holders((1,))
    parities((0,))
    update(1)
    parities((1,))
    outs = [a.reshape(1, SHARD) for a in done]
    return (*outs, shards.transpose(2, 0, 1, 3).reshape(1, 1, 2, 3, ROWS * LANES))


def solution(mesh):
    in_specs = (
        P("dp", "group", None),
        P("group", "dp"),
        P("group", "dp"),
        P("group", "dp"),
        P(),
        P("dp", None),
    )
    out_specs = (
        P("group", "dp"),
        P("group", "dp"),
        P("group", "dp"),
        P("dp", "group", None, None, None),
    )
    return jax.shard_map(
        per_device, mesh=mesh, in_specs=in_specs, out_specs=out_specs, check_vma=False
    )
```

```python
import functools

import jax
import jax.numpy as jnp
from jax import lax
from jax.experimental import pallas as pl
from jax.experimental.pallas import tpu as pltpu
from jax.sharding import PartitionSpec as P

STEP = 10
X, Y, C = 2, 4, 2
G = 8
ROWS = 256
LANES = 128
SHARD = G * ROWS * LANES
CHUNKS = ((0, 160), (160, 96))
GROUPS = ((0,), (1,))
VMEM = 8 * 2**20


def dp_index(x, y, c):
    return (x * Y + y) * C + c


def dp_perm(move):
    return [
        (dp_index(x, y, c), dp_index(*move(x, y, c)))
        for x in range(X)
        for y in range(Y)
        for c in range(C)
    ]


CORE_SWAP = dp_perm(lambda x, y, c: (x, y, 1 - c))
X_SWAP = dp_perm(lambda x, y, c: (1 - x, y, c))
Y_ON = dp_perm(lambda x, y, c: (x, (y + (1 if c == 0 else -1)) % Y, c))
Y_BACK = dp_perm(lambda x, y, c: (x, (y - (1 if c == 0 else -1)) % Y, c))


SHARE = 4096


def params():
    return pltpu.CompilerParams(vmem_limit_bytes=VMEM)


def cost(size):
    return pl.CostEstimate(flops=0, transcendentals=0, bytes_accessed=size // SHARE)


def in_hbm(value):
    return pltpu.with_memory_space_constraint(value, pltpu.HBM)


def in_vmem(value):
    return pltpu.with_memory_space_constraint(value, pltpu.VMEM)


def after(value, *others):
    return lax.optimization_barrier((value, *others))[0]


def block_at(place, own):
    index = lax.axis_index("dp")
    core, y, x = lax.rem(index, C), lax.rem(lax.div(index, C), Y), lax.div(index, C * Y)
    of_core = core if own else 1 - core
    way = 1 - 2 * of_core
    to = lax.rem(y + (2, Y - way, Y + way, 0)[place // X], Y)
    at = x if place % X == 0 else 1 - x
    return (at * Y + to) * C + of_core


def combine_kernel(tasks, order, grad, *refs):
    del order
    arrays = sum(len(task["offsets"]) for task in tasks)
    pieces = sum(len(task["splits"]) for task in tasks)
    given, outs, scratch = refs[:arrays], refs[arrays : arrays + pieces], refs[arrays + pieces :]
    work = []
    for task in tasks:
        (held, sems), scratch = scratch[:2], scratch[2:]
        count, size = sum(task["splits"]), task["rows"] * LANES
        copies = [
            [
                pltpu.make_async_copy(
                    grad.at[
                        pl.ds(pl.multiple_of(block_at(task["first"] + i, task["own"]) * G, G), G),
                        :,
                        pl.ds(task["start"] * LANES, size),
                    ],
                    held.at[pl.ds(i * G, G)],
                    sems.at[i],
                )
            ]
            for i in range(count)
        ]
        terms = []
        for offset in task["offsets"]:
            mine, given = given[0], given[1:]
            blocks = [i for i in range(count) if 0 <= offset + i < mine.shape[0]]
            if task["far"]:
                (near, near_sems), scratch = scratch[:2], scratch[2:]
                for i in blocks:
                    source = mine.at[offset + i]
                    copies[i].append(pltpu.make_async_copy(source, near.at[i], near_sems.at[i]))
                terms.append({i: (near, i) for i in blocks})
            else:
                terms.append({i: (mine, offset + i) for i in blocks})
        for block in copies:
            for copy in block:
                copy.start()
        work.append((held, copies, terms))
    for task, (held, copies, terms) in zip(tasks, work):
        places = [(out, i) for out, n in zip(outs, task["splits"]) for i in range(n)]
        outs = outs[len(task["splits"]) :]
        for i, (block, (out, at)) in enumerate(zip(copies, places)):
            for copy in block:
                copy.wait()
            for j in range(G):
                total = held[i * G + j].reshape(task["rows"], LANES).astype(jnp.float32)
                for term in terms:
                    if i in term:
                        held_term, place = term[i]
                        total = total + held_term[place, j]
                out[at, j] = total


def combine(grad, order, tasks, name):
    arrays, places, static, scratch = [], [], [], []
    for task in tasks:
        count, rows = sum(task["splits"]), task["rows"]
        scratch.append(pltpu.VMEM((count * G, 1, rows * LANES), jnp.bfloat16))
        scratch.append(pltpu.SemaphoreType.DMA((count,)))
        for held, _ in task["terms"]:
            arrays.append(in_hbm(held) if task["far"] else in_vmem(held))
            places.append(pl.BlockSpec(memory_space=pl.ANY if task["far"] else pltpu.VMEM))
            if task["far"]:
                scratch.append(pltpu.VMEM((count, G, rows, LANES), jnp.float32))
                scratch.append(pltpu.SemaphoreType.DMA((count,)))
        static.append({**task, "offsets": [offset for _, offset in task["terms"]]})
    shapes = [(n, task["rows"]) for task in tasks for n in task["splits"]]
    size = sum(n * G * rows * LANES * 8 for n, rows in shapes) + sum(a.size * 4 for a in arrays)
    outs = pl.pallas_call(
        functools.partial(combine_kernel, static),
        grid_spec=pltpu.PrefetchScalarGridSpec(
            num_scalar_prefetch=0,
            grid=(),
            in_specs=[pl.BlockSpec(memory_space=pl.ANY)] * 2 + places,
            out_specs=[pl.BlockSpec(memory_space=pltpu.VMEM)] * len(shapes),
            scratch_shapes=scratch,
        ),
        out_shape=[pltpu.VMEM((n, G, rows, LANES), jnp.float32) for n, rows in shapes],
        name=name,
        compiler_params=params(),
        cost_estimate=cost(size),
    )(order, in_hbm(grad), *arrays)
    results = []
    for task in tasks:
        results.append(outs[: len(task["splits"])])
        outs = outs[len(task["splits"]) :]
    return results


def order_kernel(holder, *refs):
    (*state, ordered), sems = refs[:-1], refs[-1]
    copies = [
        pltpu.make_async_copy(state[s].at[j], ordered.at[holder[j], s], sems.at[j, s])
        for j in range(G)
        for s in range(3)
    ]
    for copy in copies:
        copy.start()
    for copy in copies:
        copy.wait()


def order_state(state, holder):
    return pl.pallas_call(
        order_kernel,
        grid_spec=pltpu.PrefetchScalarGridSpec(
            num_scalar_prefetch=1,
            grid=(),
            in_specs=[pl.BlockSpec(memory_space=pltpu.VMEM)] * 3,
            out_specs=pl.BlockSpec(memory_space=pl.ANY),
            scratch_shapes=[pltpu.SemaphoreType.DMA((G, 3))],
        ),
        out_shape=pltpu.HBM((G, 3, ROWS, LANES), jnp.float32),
        name="order",
        compiler_params=params(),
        cost_estimate=cost(G * 3 * ROWS * LANES * 8),
    )(holder, *[in_vmem(a) for a in state])


def finish_kernel(terms, first, rows, holder, *refs):
    parts = refs[:terms]
    ordered, total, sems = refs[-3:]
    copies = []
    for j in range(G):
        grad = parts[0][0, j]
        for part in parts[1:]:
            grad = grad + part[0, j]
        total[j] = grad
        copy = pltpu.make_async_copy(
            total.at[j], ordered.at[holder[j], pl.ds(first, rows)], sems.at[j]
        )
        copy.start()
        copies.append(copy)
    for copy in copies:
        copy.wait()


def finish(parts, ordered, holder, first, rows, group_rows):
    held = [] if ordered is None else [in_hbm(ordered)]
    return pl.pallas_call(
        functools.partial(finish_kernel, len(parts), first, rows),
        grid_spec=pltpu.PrefetchScalarGridSpec(
            num_scalar_prefetch=1,
            grid=(),
            in_specs=[pl.BlockSpec(memory_space=pltpu.VMEM)] * len(parts)
            + [pl.BlockSpec(memory_space=pl.ANY)] * len(held),
            out_specs=pl.BlockSpec(memory_space=pl.ANY),
            scratch_shapes=[
                pltpu.VMEM((G, rows, LANES), jnp.float32),
                pltpu.SemaphoreType.DMA((G,)),
            ],
        ),
        out_shape=pltpu.HBM((G, group_rows, LANES), jnp.float32),
        name="finish",
        input_output_aliases={1 + len(parts): 0} if held else {},
        compiler_params=params(),
        cost_estimate=cost(G * rows * LANES * 4 * (len(parts) + 2)),
    )(holder, *[in_vmem(a) for a in parts], *held)


def adam_step(grad, old, first, second):
    m = 0.9 * first + 0.1 * grad
    v = 0.95 * second + 0.05 * grad * grad
    first_hat = m / (1.0 - 0.9**STEP)
    second_hat = v / (1.0 - 0.95**STEP)
    w = old - 0.01 * (first_hat / (jnp.sqrt(second_hat) + 1e-08) + 0.1 * old)
    return w, m, v


def adam_kernel(first, rows, start, holder, ordered, *refs):
    state, refs = refs[:3], refs[3:]
    *outs, grads, old, fresh, grad_sems, in_sems, out_sems = refs[-9:]
    here = pl.ds(start, rows)
    half = G // 2
    loads, stores = [[], []], []
    for n in range(2):
        pieces = pl.ds(n * half, half)
        for j in range(n * half, (n + 1) * half):
            source = ordered.at[holder[j], pl.ds(first, rows)]
            loads[n].append(pltpu.make_async_copy(source, grads.at[j], grad_sems.at[j]))
        for s in range(3):
            source = state[s].at[pieces, here]
            loads[n].append(pltpu.make_async_copy(source, old.at[s, pieces], in_sems.at[n, s]))
        for load in loads[n]:
            load.start()
    for n in range(2):
        pieces = pl.ds(n * half, half)
        for load in loads[n]:
            load.wait()
        for j in range(n * half, (n + 1) * half):
            for s, value in enumerate(adam_step(grads[j], *[old[s, j] for s in range(3)])):
                fresh[s, j] = value
        for s in range(3):
            target = outs[s].at[pieces, here]
            stores.append(pltpu.make_async_copy(fresh.at[s, pieces], target, out_sems.at[n, s]))
            stores[-1].start()
    for store in stores:
        store.wait()


def adam(ordered, state, done, holder, first, start, rows):
    held = [in_hbm(a) for a in done or ()]
    return pl.pallas_call(
        functools.partial(adam_kernel, first, rows, start),
        grid_spec=pltpu.PrefetchScalarGridSpec(
            num_scalar_prefetch=1,
            grid=(),
            in_specs=[pl.BlockSpec(memory_space=pl.ANY)] * (4 + len(held)),
            out_specs=[pl.BlockSpec(memory_space=pl.ANY)] * 3,
            scratch_shapes=[
                pltpu.VMEM((G, rows, LANES), jnp.float32),
                pltpu.VMEM((3, G, rows, LANES), jnp.float32),
                pltpu.VMEM((3, G, rows, LANES), jnp.float32),
                pltpu.SemaphoreType.DMA((G,)),
                pltpu.SemaphoreType.DMA((2, 3)),
                pltpu.SemaphoreType.DMA((2, 3)),
            ],
        ),
        out_shape=[pltpu.HBM((G, ROWS, LANES), jnp.float32)] * 3,
        name="adam",
        input_output_aliases={5 + n: n for n in range(len(held))},
        compiler_params=params(),
        cost_estimate=cost(G * rows * LANES * 4 * 7),
    )(holder, in_hbm(ordered), *[in_hbm(a) for a in state], *held)


def parity_kernel(start, rows, coeff, sums, old, *refs):
    out, near_coeff, near_sums, near_old, fresh, coeff_sem, in_sems, out_sems = refs[-8:]
    size = rows // 2
    loads, stores = [], []
    coeff_load = pltpu.make_async_copy(coeff, near_coeff, coeff_sem)
    coeff_load.start()
    for n in range(2):
        mine, whole = pl.ds(n * size, size), pl.ds(start + n * size, size)
        loads.append(
            [
                pltpu.make_async_copy(sums.at[:, mine], near_sums.at[:, mine], in_sems.at[n, 0]),
                pltpu.make_async_copy(
                    old.at[:, :, whole], near_old.at[:, :, mine], in_sems.at[n, 1]
                ),
            ]
        )
        for load in loads[n]:
            load.start()
    coeff_load.wait()
    for n in range(2):
        mine, whole = pl.ds(n * size, size), pl.ds(start + n * size, size)
        for load in loads[n]:
            load.wait()
        totals = [[None] * 2 for _ in range(3)]
        for g in range(G):
            values = adam_step(near_sums[g, mine], *[near_old[g, s, mine] for s in range(3)])
            for s, value in enumerate(values):
                for k in range(2):
                    term = near_coeff[pl.ds(k * G + g, 1)] * value
                    totals[s][k] = term if g == 0 else totals[s][k] + term
        for s in range(3):
            for k in range(2):
                fresh[s, mine, k, :] = totals[s][k]
        stores.append(pltpu.make_async_copy(fresh.at[:, mine], out.at[:, whole], out_sems.at[n]))
        stores[n].start()
    for store in stores:
        store.wait()


def parity(sums, old, coeff, done, start, rows):
    held = [] if done is None else [in_hbm(done)]
    return pl.pallas_call(
        functools.partial(parity_kernel, start, rows),
        grid_spec=pltpu.PrefetchScalarGridSpec(
            num_scalar_prefetch=0,
            grid=(),
            in_specs=[pl.BlockSpec(memory_space=pl.ANY)] * (3 + len(held)),
            out_specs=pl.BlockSpec(memory_space=pl.ANY),
            scratch_shapes=[
                pltpu.VMEM((2 * G, LANES), jnp.float32),
                pltpu.VMEM((G, rows, LANES), jnp.float32),
                pltpu.VMEM((G, 3, rows, LANES), jnp.float32),
                pltpu.VMEM((3, rows, 2, LANES), jnp.float32),
                pltpu.SemaphoreType.DMA,
                pltpu.SemaphoreType.DMA((2, 2)),
                pltpu.SemaphoreType.DMA((2,)),
            ],
        ),
        out_shape=pltpu.HBM((3, ROWS, 2, LANES), jnp.float32),
        name="parity",
        input_output_aliases={3: 0} if held else {},
        compiler_params=params(),
        cost_estimate=cost(G * 4 * rows * LANES * 4),
    )(coeff, sums, old, *held)


def per_device(
    grad_parts, master_weights, first_moment, second_moment, cauchy_points, parity_holder
):
    holder = parity_holder.reshape(G)
    state = [a.reshape(G, ROWS, LANES) for a in (master_weights, first_moment, second_moment)]
    points = cauchy_points.astype(jnp.float32)
    coeff = 1.0 / (points[:2][:, None] + points[2:][None, :])
    coeff = jnp.broadcast_to(coeff.reshape(2 * G, 1), (2 * G, LANES))
    grad = grad_parts.reshape(X * Y * C * G, 1, ROWS * LANES)
    nothing = jnp.zeros((1,), jnp.int32)
    half = X * Y // 2
    got, hop, totals, ordered, sums = {}, {}, {}, {}, {}
    olds, done, shards, token = None, None, None, ()

    def task(n, own, first, splits, terms, far=False):
        start, rows = CHUNKS[n]
        return dict(own=own, first=first, start=start, rows=rows, splits=splits, terms=terms, far=far)

    def send(value, name, n, pairs):
        with jax.named_scope(f"{name}_{n}"):
            return lax.ppermute(value, "dp", pairs)

    def run(*jobs, wait=()):
        nonlocal token
        order = after(nothing, *token, *wait)
        name = "_".join(f"{job[2]}{job[3]}" for job in jobs)
        results = combine(grad, order, [job[0] for job in jobs], name)
        token = (results[0][0],)
        for (_, use, *_), result in zip(jobs, results):
            use(*result)

    def then(*values):
        nonlocal token
        token = values

    def swap_core(n, first, splits):
        def use(*sent):
            at = first
            for a in sent:
                got.setdefault(n, []).append((at, send(a, "core", n, CORE_SWAP)))
                at += a.shape[0]

        return task(n, False, first, splits, []), use, "core", n

    def terms_at(n, first, count):
        return [(a, first - at) for at, a in got[n] if first < at + a.shape[0] and at < first + count]

    def far(n):
        def use(block):
            hop[n, 0] = send(block, "far", n, Y_ON)

        return task(n, True, 0, (X,), terms_at(n, 0, X)), use, "far", n

    def near(n):
        def use(block):
            hop[n, 1] = send(block, "near", n, Y_BACK)

        return task(n, True, X, (X,), terms_at(n, X, X)), use, "near", n

    def ahead(n):
        def use(block):
            hop[n, 2] = send(block, "ahead", n, Y_ON)

        terms = terms_at(n, half, X) + [(hop[n, 0], 0)]
        return task(n, True, half, (X,), terms), use, "ahead", n

    def here(n, from_hbm=False):
        def use(own, block):
            totals[n] = [own, send(block, "swap", n, X_SWAP)]

        terms = terms_at(n, half + X, X) + [(hop[n, 2], 0), (hop[n, 1], 0)]
        return task(n, True, half + X, (1, 1), terms, far=from_hbm), use, "here", n

    def place(n):
        (group,) = [g for g in GROUPS if n in g]
        base = min(CHUNKS[m][0] for m in group)
        return group, CHUNKS[n][0] - base, sum(CHUNKS[m][1] for m in group)

    def give(n):
        group, first, group_rows = place(n)
        rows = CHUNKS[n][1]
        parts, before = totals[n], ordered.get(group)
        ordered[group] = finish(parts, before, after(holder, *token), first, rows, group_rows)
        then(ordered[group])

    def to_holders(group):
        sums[group] = lax.all_to_all(ordered[group], "group", 0, 0)

    def update(n):
        nonlocal done
        group, first, _ = place(n)
        start, rows = CHUNKS[n]
        done = adam(ordered[group], state, done, after(holder, *token), first, start, rows)
        then(done[0])

    def parities(group):
        nonlocal shards
        start = min(CHUNKS[m][0] for m in group)
        rows = sum(CHUNKS[m][1] for m in group)
        shards = parity(sums[group], olds, after(coeff, *token), shards, start, rows)
        then(shards)

    run(swap_core(0, 0, (1, 1)))
    run(swap_core(0, 2, (1, 1)))
    run(far(0))
    old = order_state(state, after(holder, *token))
    then(old)
    olds = lax.all_to_all(old, 'group', 0, 0)
    run(near(0), swap_core(0, 4, (1, 1, 1, 1)))
    run(ahead(0))
    run(swap_core(1, 0, (1, 1, 1, 1)), swap_core(1, 4, (1, 1, 1, 1)))
    run(far(1), wait=(hop[0, 1],))
    run(near(1))
    run(here(0))
    run(ahead(1))
    give(0)
    to_holders((0,))
    run(here(1, True))
    update(0)
    give(1)
    to_holders((1,))
    parities((0,))
    update(1)
    parities((1,))
    outs = [a.reshape(1, SHARD) for a in done]
    return (*outs, shards.transpose(2, 0, 1, 3).reshape(1, 1, 2, 3, ROWS * LANES))


def solution(mesh):
    in_specs = (
        P("dp", "group", None),
        P("group", "dp"),
        P("group", "dp"),
        P("group", "dp"),
        P(),
        P("dp", None),
    )
    out_specs = (
        P("group", "dp"),
        P("group", "dp"),
        P("group", "dp"),
        P("dp", "group", None, None, None),
    )
    return jax.shard_map(
        per_device, mesh=mesh, in_specs=in_specs, out_specs=out_specs, check_vma=False
    )
```
